512 devices in a mesh: ctx: 64 (over y, z), head: 8 (over x, core).
Axes of the slice: x: 4, y: 4, z: 16, core: 2. Of those that a mesh axis runs over, the one named last changes fastest.
Arguments:
- queries: bfloat16 [16384, 4096], P('ctx', 'head'), may hold values from -200 to 200
- span_keys: bfloat16 [16384, 4096], P('ctx', 'head'), may hold values from -6 to 6
- span_values: bfloat16 [16384, 4096], P('ctx', 'head'), may hold values from -96 to 96
- cache_keys: bfloat16 [65536, 4096], P('ctx', 'head'), may hold values from -6 to 6
- cache_values: bfloat16 [65536, 4096], P('ctx', 'head'), may hold values from -96 to 96
- land_keys: bfloat16 [1024, 4096], P('ctx', 'head'), may hold values from -4.5 to 4.5
- land_values: bfloat16 [1024, 4096], P('ctx', 'head'), may hold values from -96 to 96
- out_weight: bfloat16 [4096, 4096], P('head', 'ctx'), may hold values from -0.09375 to 0.09375
- selection: int32 [256, 32, 4], P('ctx', 'head'), may hold values from 0 to 1023, as said below
Outputs:
- projected: bfloat16 [16384, 4096], P('ctx', 'head')
The draws below stay inside these ranges and needn't reach their ends.
Inputs may be any that keep to these rules, and one draw needn't show every extreme that they name: `selection`: the 4 blocks of one query group and head are distinct. Count block b as owned by ctx index b // 16. Over all groups and heads of one device (one index of ctx and one of head), the selections within one owner's blocks number at most 4 and form at most 1 distinct pairs of block and head; some owner receives exactly that many of both from every device.
All inputs are finite; a program needn't handle non-finite values.
Results may differ from the reference program's by a relative error of at most 0.015.
Values may be sent and summed in bfloat16 or wider, within the bound.
A program may use at most 64 MiB of HBM per device.

```python
import math
import jax
import jax.numpy as jnp
from jax import lax

D = 4096
HEADS = 32
DH = 128
BLOCK = 64
TOPB = 4
BLK_DEV = 16
G_DEV = 4
SPAN = 16384
NCTX = 65536
NBLK = 1024
NGROUP = 256
N_CTX = 64
N_HEAD = 8


def shared_fields(key):
    base_key = jax.random.fold_in(key, 4099)
    land_key = jax.random.fold_in(base_key, 0)
    query_key = jax.random.fold_in(base_key, 1)
    span_key = jax.random.fold_in(base_key, 3)
    full_width = HEADS * DH
    landmark = jnp.clip(jax.random.normal(land_key, (NBLK, full_width), jnp.float32), -4.5, 4.5)
    query_rows = jnp.clip(jax.random.normal(query_key, (SPAN, full_width), jnp.float32), -6.0, 6.0)
    span_rows = jnp.clip(jax.random.normal(span_key, (SPAN, full_width), jnp.float32), -6.0, 6.0)
    return (query_rows, landmark, span_rows)


def draw_queries(key, part):
    query_rows, landmark, span_rows = shared_fields(key)
    return query_rows.astype(jnp.bfloat16)


def draw_land_keys(key, part):
    query_rows, landmark, span_rows = shared_fields(key)
    return landmark.astype(jnp.bfloat16)


def draw_span_keys(key, part):
    query_rows, landmark, span_rows = shared_fields(key)
    return span_rows.astype(jnp.bfloat16)


def device_picks(subkey, popular):
    head_dev = HEADS // N_HEAD
    candidate_count = 2 * TOPB
    slot_most = (head_dev * candidate_count + N_CTX - 1) // N_CTX
    pool_size = N_CTX * slot_most
    prio_key, owner_key, first_key, rest_key, group_key = jax.random.split(subkey, 5)
    pool_owner = jnp.arange(pool_size, dtype=jnp.int32) // slot_most
    pool_rank = jnp.arange(pool_size, dtype=jnp.int32) % slot_most
    priority = jax.random.randint(prio_key, (pool_size,), 0, 4096, dtype=jnp.int32)
    priority = priority + pool_owner * 4096 // max(N_CTX - 1, 1)
    priority = priority + jnp.where(pool_owner == popular, 1 << 16, 0).astype(jnp.int32)
    priority = priority * pool_size + jnp.arange(pool_size, dtype=jnp.int32)
    chosen = lax.top_k(priority, head_dev * candidate_count)[1].astype(jnp.int32)
    leading = jax.random.permutation(first_key, chosen[:head_dev])
    trailing = jax.random.permutation(rest_key, chosen[head_dev:]).reshape(head_dev, candidate_count - 1)
    slot_table = jnp.concatenate([leading[:, None], trailing], axis=1)
    owner_base = jax.random.randint(owner_key, (N_CTX,), 0, BLK_DEV, dtype=jnp.int32)
    cand_owner = pool_owner[slot_table]
    local_block = (owner_base[cand_owner] + pool_rank[slot_table]) % BLK_DEV
    candidates = cand_owner * BLK_DEV + local_block
    group_keys = jax.random.split(group_key, G_DEV * head_dev)
    head_list = jnp.tile(jnp.arange(head_dev, dtype=jnp.int32), G_DEV)

    def one_group(pick_key, head_index):
        order_key, shuffle_key = jax.random.split(pick_key)
        others = jax.random.permutation(order_key, candidate_count - 1)[:TOPB - 1].astype(jnp.int32) + 1
        picked = jnp.concatenate([jnp.zeros((1,), jnp.int32), others])
        picked = jax.random.permutation(shuffle_key, picked)
        return candidates[head_index, picked]
    return jax.vmap(one_group)(group_keys, head_list).reshape(G_DEV, head_dev, TOPB)


def draw_selection(key, part):
    base_key = jax.random.fold_in(key, 7919)
    popular_key, device_key = jax.random.split(base_key)
    popular = jax.random.randint(popular_key, (), 0, N_CTX, dtype=jnp.int32)
    device_keys = jax.random.split(device_key, N_CTX * N_HEAD)
    picked = jax.vmap(lambda subkey: device_picks(subkey, popular))(device_keys)
    head_dev = HEADS // N_HEAD
    picked = picked.reshape(N_CTX, N_HEAD, G_DEV, head_dev, TOPB).transpose(0, 2, 1, 3, 4)
    return picked.reshape(NGROUP, HEADS, TOPB).astype(jnp.int32)


def block_levels(stream_key, dims, cuts, low, top_value):
    loudness, own = 1.0, jax.random.fold_in(stream_key, 6)
    for dim, shards_of in cuts:
        steps = jnp.exp(jax.random.uniform(jax.random.fold_in(own, dim), (shards_of,), jnp.float32, low / len(cuts), top_value / len(cuts)))
        loudness = loudness * jnp.repeat(steps, dims[dim] // shards_of).reshape([-1 if axis == dim else 1 for axis in range(len(dims))])
    return loudness


def gaussian(key, extent, scale, most, cuts=(), kind=jnp.bfloat16):
    factor_of = block_levels(key, extent, cuts, -0.22, 0.18) if cuts else 1.0
    entries = jax.random.normal(key, extent, jnp.float32) * scale * factor_of
    return jnp.minimum(jnp.maximum(entries, -most), most).astype(kind)


def setup_inputs(seed: int = 0) -> dict:
    arg_keys = jax.random.split(jax.random.key(seed), 10)
    queries = draw_queries(jax.random.fold_in(arg_keys[9], 71), 0)
    span_keys = draw_span_keys(jax.random.fold_in(arg_keys[9], 71), 0)
    span_values = gaussian(arg_keys[2], (SPAN, HEADS * DH), 16.0, 96.0, ((0, 64), (1, 8)))
    cache_keys = gaussian(arg_keys[3], (NCTX, HEADS * DH), 1.0, 6.0, ((0, 64), (1, 8)))
    cache_values = gaussian(arg_keys[4], (NCTX, HEADS * DH), 16.0, 96.0, ((0, 64), (1, 8)))
    land_keys = draw_land_keys(jax.random.fold_in(arg_keys[9], 71), 0)
    land_values = gaussian(arg_keys[6], (NBLK, HEADS * DH), 16.0, 96.0, ((0, 64), (1, 8)))
    out_weight = gaussian(arg_keys[7], (HEADS * DH, D), (HEADS * DH) ** -0.5, 0.09375, ((0, 8), (1, 64)))
    selection = draw_selection(jax.random.fold_in(arg_keys[9], 71), 0)
    return dict(queries=queries, span_keys=span_keys, span_values=span_values, cache_keys=cache_keys, cache_values=cache_values, land_keys=land_keys, land_values=land_values, out_weight=out_weight, selection=selection)


def reference(queries, span_keys, span_values, cache_keys, cache_values, land_keys, land_values, out_weight, selection):
    scaling = 1.0 / math.sqrt(DH)
    groups = SPAN // BLOCK
    causal = jnp.arange(BLOCK)[:, None] >= jnp.arange(BLOCK)[None, :]
    highest = lax.Precision.HIGHEST

    def rounded(weights):
        return lax.optimization_barrier(weights.astype(jnp.bfloat16)).astype(jnp.float32)

    def one_head(head_index):

        def column_cut(source):
            return lax.dynamic_slice_in_dim(source, head_index * DH, DH, 1).astype(jnp.float32)
        query_head = column_cut(queries).reshape(groups, BLOCK, DH)
        land_scores = jnp.einsum('gqd,nd->gqn', query_head, column_cut(land_keys), precision=highest) * scaling
        picked = lax.dynamic_index_in_dim(selection, head_index, 1, keepdims=False)
        key_blocks = column_cut(cache_keys).reshape(NBLK, BLOCK * DH)[picked].reshape(groups, TOPB * BLOCK, DH)
        value_blocks = column_cut(cache_values).reshape(NBLK, BLOCK * DH)[picked].reshape(groups, TOPB * BLOCK, DH)
        chosen_scores = jnp.einsum('gqd,gkd->gqk', query_head, key_blocks, precision=highest) * scaling
        local_keys = column_cut(span_keys).reshape(groups, BLOCK, DH)
        local_values = column_cut(span_values).reshape(groups, BLOCK, DH)
        local_scores = jnp.einsum('gqd,gkd->gqk', query_head, local_keys, precision=highest) * scaling
        local_scores = jnp.where(causal[None], local_scores, -jnp.inf)
        top = jnp.maximum(jnp.maximum(lax.optimization_barrier(jnp.max(land_scores, axis=2)), lax.optimization_barrier(jnp.max(chosen_scores, axis=2))), lax.optimization_barrier(jnp.max(local_scores, axis=2)))
        land_weights = jnp.exp(land_scores - top[:, :, None])
        chosen_weights = jnp.exp(chosen_scores - top[:, :, None])
        local_weights = jnp.exp(local_scores - top[:, :, None])
        summed_weights = lax.optimization_barrier(jnp.sum(land_weights, axis=2)) + lax.optimization_barrier(jnp.sum(chosen_weights, axis=2)) + lax.optimization_barrier(jnp.sum(local_weights, axis=2))
        numerator = jnp.einsum('gqn,nd->gqd', rounded(land_weights), column_cut(land_values), precision=highest)
        numerator = numerator + jnp.einsum('gqk,gkd->gqd', rounded(chosen_weights), value_blocks, precision=highest)
        numerator = numerator + jnp.einsum('gqk,gkd->gqd', rounded(local_weights), local_values, precision=highest)
        return (numerator / summed_weights[:, :, None]).reshape(SPAN, DH).astype(jnp.bfloat16)
    heads_out = lax.map(one_head, jnp.arange(HEADS, dtype=jnp.int32))
    attended = jnp.transpose(heads_out, (1, 0, 2)).reshape(SPAN, HEADS * DH)
    head_width = HEADS // N_HEAD * DH
    summed = jnp.zeros((SPAN, D), jnp.float32)
    for head_shard in range(N_HEAD):
        rows_in = attended[:, head_shard * head_width:(head_shard + 1) * head_width].astype(jnp.float32)
        rows_weight = out_weight[head_shard * head_width:(head_shard + 1) * head_width].astype(jnp.float32)
        partial_value = jnp.dot(rows_in, rows_weight, precision=highest)
        summed = summed + rounded(partial_value)
    return summed.astype(jnp.bfloat16)
```

```python
import functools
import math

import jax
import jax.numpy as jnp
from jax import lax
from jax.experimental import pallas as pl
from jax.experimental.pallas import tpu as pltpu
from jax.sharding import PartitionSpec as P

MESH = pl.DeviceIdType.MESH
BLOCK = 64
NY, NZ, NX = 4, 16, 4
NCTX = NY * NZ
GROUPS, HEADS, PICKS, DH = 4, 4, 4, 128
ROWS, WIDTH = GROUPS * BLOCK, HEADS * DH
LAND = 16
BLOCKS = 16
STEPS = NZ // 2
NT = (((1,), (1,)), ((), ()))
SCALE = 1.0 / math.sqrt(DH)


def offsets(i):
    k, dy = lax.div(i, 4), lax.rem(i, 4)
    odd = lax.rem(k, 2)
    dz = lax.rem(odd * lax.div(k + 1, 2) + (1 - odd) * (NZ - lax.div(k, 2)), NZ)
    return dy, dz


def slot_of(dy, dz):
    k = jnp.where(dz == 0, 0, jnp.where(dz <= 8, 2 * dz - 1, 2 * (NZ - dz)))
    return 4 * k + dy


def slots_of(picks):
    ctx = lax.axis_index("ctx")
    owner = picks >> 4
    return slot_of(((ctx >> 4) - (owner >> 4)) & 3, ((ctx & 15) - (owner & 15)) & 15)


def remote(src, dst, send, recv, ctx, head):
    return pltpu.make_async_remote_copy(
        src_ref=src,
        dst_ref=dst,
        send_sem=send,
        recv_sem=recv,
        device_id=(ctx, head),
        device_id_type=MESH,
    )


def kernel(
    slots,
    pick_row,
    q,
    sk,
    sv,
    ck,
    cv,
    land,
    wt,
    out,
    pick_all,
    code_v,
    code_s,
    land_all,
    w_lane,
    w_all,
    send_k,
    send_v,
    recv_k,
    recv_v,
    att,
    prob,
    acc,
    top,
    tot,
    sums,
    pair_k,
    pair_v,
    pick_sem,
    code_sem,
    land_s,
    land_r,
    swap_sem,
    wz_s,
    wz_r,
    core_sem,
    yl_s,
    yl_r,
    yw_s,
    yw_r,
    kv_s,
    kv_r,
    mate_s,
    mate_r,
    xs_s,
    xs_r,
    fwd_s,
    fwd_r,
    far_s,
    far_r,
    ffw_s,
    ffw_r,
):
    ctx, head = lax.axis_index("ctx"), lax.axis_index("head")
    y, z = lax.div(ctx, NZ), lax.rem(ctx, NZ)
    x, core = lax.div(head, 2), lax.rem(head, 2)
    mate = 2 * x + 1 - core
    x_up, x_dn = lax.rem(x + 1, NX), lax.rem(x + NX - 1, NX)
    x_far = lax.rem(x + 2, NX)
    y_up, y_dn = lax.rem(y + 1, NY), lax.rem(y + NY - 1, NY)
    y_far = lax.rem(y + 2, NY)
    z_up = y * NZ + lax.rem(z + 1, NZ)
    z_dn = y * NZ + lax.rem(z + NZ - 1, NZ)
    swap_ctx, swap_head = x * NZ + z, 2 * y + core
    off_diag = x != y

    def peer(i):
        dy, dz = offsets(i)
        return lax.rem(y + dy, NY) * NZ + lax.rem(z + dz, NZ)

    barrier = pltpu.get_barrier_semaphore()

    def greet(i, carry):
        pl.semaphore_signal(
            barrier, inc=1, device_id=(peer(i), head), device_id_type=MESH
        )
        return carry

    lax.fori_loop(1, NCTX, greet, 0)
    for h in (mate, 2 * x_up + core, 2 * x_dn + core):
        pl.semaphore_signal(barrier, inc=1, device_id=(ctx, h), device_id_type=MESH)

    @pl.when(off_diag)
    def _():
        pl.semaphore_signal(
            barrier, inc=1, device_id=(swap_ctx, swap_head), device_id_type=MESH
        )

    land_all[ctx] = land[...]

    @pl.when(x == y)
    def _():
        w_lane[z] = wt[...]

    def split(b, carry):
        rows = pl.ds(pl.multiple_of(b * BLOCK, BLOCK), BLOCK)
        for h in range(HEADS):
            pair_k[b * HEADS + h] = ck[rows, h * DH : (h + 1) * DH]
            pair_v[b * HEADS + h] = cv[rows, h * DH : (h + 1) * DH]
        return carry

    lax.fori_loop(0, BLOCKS, split, 0)

    pl.semaphore_wait(barrier, NCTX - 1 + 3 + jnp.where(off_diag, 1, 0))

    def ring(buf, base, s, d, send, recv):
        slot = base + lax.rem(z + (NZ - s if d == 0 else s), NZ)
        return remote(
            buf.at[slot],
            buf.at[slot],
            send.at[d, s],
            recv.at[d, s],
            z_up if d == 0 else z_dn,
            head,
        )

    def ring_in(buf, base, s, d, send, recv):
        slot = base + lax.rem(z + (NZ - s - 1 if d == 0 else s + 1), NZ)
        return remote(
            buf.at[slot],
            buf.at[slot],
            send.at[d, s],
            recv.at[d, s],
            z_up if d == 0 else z_dn,
            head,
        )

    land_ring = functools.partial(ring, land_all, y * NZ)
    land_in = functools.partial(ring_in, land_all, y * NZ)
    w_ring = functools.partial(ring, w_lane, 0)
    w_in = functools.partial(ring_in, w_lane, 0)
    for d in (0, 1):
        land_ring(0, d, land_s, land_r).start()
    swap = remote(
        wt, w_lane.at[z], swap_sem.at[0], swap_sem.at[1], swap_ctx, swap_head
    )

    @pl.when(off_diag)
    def _():
        swap.start()

    own_picks = pltpu.make_async_copy(pick_row, pick_all.at[ctx], pick_sem.at[1])
    own_picks.start()

    def tell(i, carry):
        remote(
            pick_row,
            pick_all.at[ctx],
            pick_sem.at[0],
            pick_sem.at[1],
            peer(i),
            head,
        ).start()
        return carry

    lax.fori_loop(1, NCTX, tell, 0)

    @pl.when(off_diag)
    def _():
        swap.wait_recv()

    for d in (0, 1):
        w_ring(0, d, wz_s, wz_r).start()
    pltpu.make_async_copy(pick_all, pick_all, pick_sem.at[1]).wait()
    asked = pick_all[:, 0, :]
    lane = lax.broadcasted_iota(jnp.int32, asked.shape, 1)
    mine = jnp.logical_and(lane < GROUPS * HEADS * PICKS, (asked >> 4) == ctx)
    code = jnp.where(mine, (asked & 15) * HEADS + ((lane >> 2) & 3), 0)
    code = jnp.max(code, axis=1, keepdims=True)
    code_v[...] = jnp.broadcast_to(code, code_v.shape)
    to_scalar = pltpu.make_async_copy(code_v, code_s, code_sem.at[0])
    to_scalar.start()
    to_scalar.wait()

    def block_for(cache, t):
        return cache[code_s[t, 0]]

    recv_k[0] = block_for(pair_k, ctx)
    recv_v[0] = block_for(pair_v, ctx)

    def send_block(cache, out_buf, in_buf, which, i, carry):
        t = peer(i)
        out_buf[i] = block_for(cache, t)
        remote(
            out_buf.at[i], in_buf.at[i], kv_s.at[which], kv_r.at[which], t, head
        ).start()
        return carry

    send_key = functools.partial(send_block, pair_k, send_k, recv_k, 0)
    send_value = functools.partial(send_block, pair_v, send_v, recv_v, 1)

    edges = [1 + (NCTX - 1) * s // STEPS for s in range(STEPS + 1)]
    for s in range(STEPS):
        for d in (0, 1):
            if d == 0 or s < STEPS - 1:
                land_in(s, d, land_s, land_r).wait_recv()
                nxt = s + 1
                if nxt < STEPS - d:
                    land_ring(nxt, d, land_s, land_r).start()
                w_in(s, d, wz_s, wz_r).wait_recv()
                if nxt < STEPS - d:
                    w_ring(nxt, d, wz_s, wz_r).start()
        lax.fori_loop(edges[s], edges[s + 1], send_key, 0)

    def y_copy(buf, row, half, send, recv, j, to):
        n = buf.shape[0] // NY
        part = n // 2 if half is not None else n
        at = row * n + (half * part if half is not None else 0)
        ref = buf.at[pl.ds(at, part)]
        return remote(ref, ref, send.at[j], recv.at[j], to * NZ + z, head)

    def y_first(buf, send, recv):
        return [
            y_copy(buf, y, None, send, recv, 0, y_up),
            y_copy(buf, y, None, send, recv, 1, y_dn),
        ]

    def y_first_in(buf, send, recv):
        return [
            y_copy(buf, y_dn, None, send, recv, 0, y_up),
            y_copy(buf, y_up, None, send, recv, 1, y_dn),
        ]

    def y_second(buf, send, recv):
        return [
            y_copy(buf, y_dn, 0, send, recv, 2, y_up),
            y_copy(buf, y_up, 1, send, recv, 3, y_dn),
        ]

    def y_second_in(buf, send, recv):
        return [
            y_copy(buf, y_far, 0, send, recv, 2, y_up),
            y_copy(buf, y_far, 1, send, recv, 3, y_dn),
        ]

    for c in y_first(land_all, yl_s, yl_r):
        c.start()
    half = NZ // 2
    to_mate = remote(
        w_lane.at[pl.ds((1 - core) * half, half)],
        w_all.at[pl.ds((2 * y + core) * half, half)],
        core_sem.at[0],
        core_sem.at[1],
        ctx,
        mate,
    )
    to_mate.start()
    keep = pltpu.make_async_copy(
        w_lane.at[pl.ds(core * half, half)],
        w_all.at[pl.ds((2 * y + core) * half, half)],
        core_sem.at[2],
    )
    keep.start()
    lax.fori_loop(1, NCTX, send_value, 0)
    remote(
        w_lane.at[pl.ds(core * half, half)],
        w_all.at[pl.ds((2 * y + 1 - core) * half, half)],
        core_sem.at[0],
        core_sem.at[1],
        ctx,
        mate,
    ).wait_recv()
    keep.wait()
    for c in y_first(w_all, yw_s, yw_r):
        c.start()
    for c, f in zip(
        y_first_in(land_all, yl_s, yl_r), y_second(land_all, yl_s, yl_r)
    ):
        c.wait_recv()
        f.start()
    for c in y_second_in(land_all, yl_s, yl_r):
        c.wait_recv()

    def first_part(i, carry):
        g, h = lax.div(i, HEADS), lax.rem(i, HEADS)
        rows = pl.ds(pl.multiple_of(g * BLOCK, BLOCK), BLOCK)
        cols = pl.ds(pl.multiple_of(h * DH, DH), DH)
        qv = q[rows, cols]
        lk = land_all[:, 0:LAND, cols].reshape(NCTX * LAND, DH)
        lv = land_all[:, LAND : 2 * LAND, cols].reshape(NCTX * LAND, DH)
        s_l = lax.dot_general(qv, lk, NT, preferred_element_type=jnp.float32) * SCALE
        s_s = (
            lax.dot_general(
                qv, sk[rows, cols], NT, preferred_element_type=jnp.float32
            )
            * SCALE
        )
        causal = lax.broadcasted_iota(jnp.int32, s_s.shape, 0) >= lax.broadcasted_iota(
            jnp.int32, s_s.shape, 1
        )
        s_s = jnp.where(causal, s_s, -jnp.inf)
        m = jnp.maximum(
            jnp.max(s_l, axis=1, keepdims=True), jnp.max(s_s, axis=1, keepdims=True)
        )
        p_l, p_s = jnp.exp(s_l - m), jnp.exp(s_s - m)
        total = jnp.sum(p_l, axis=1, keepdims=True) + jnp.sum(
            p_s, axis=1, keepdims=True
        )
        acc[i] = jnp.dot(
            p_l.astype(jnp.bfloat16), lv, preferred_element_type=jnp.float32
        ) + jnp.dot(
            p_s.astype(jnp.bfloat16),
            sv[rows, cols],
            preferred_element_type=jnp.float32,
        )
        top[i] = jnp.broadcast_to(m, (BLOCK, DH))
        tot[i] = jnp.broadcast_to(total, (BLOCK, DH))
        return carry

    lax.fori_loop(0, GROUPS * HEADS, first_part, 0)

    for c, f in zip(y_first_in(w_all, yw_s, yw_r), y_second(w_all, yw_s, yw_r)):
        c.wait_recv()
        f.start()
    for c in y_second_in(w_all, yw_s, yw_r):
        c.wait_recv()

    def chosen(buf, i):
        blocks = []
        for p in range(PICKS):
            blocks.append(buf[slots[i * PICKS + p]])
        return jnp.concatenate(blocks, axis=0)

    def kv_wait(buf, sem):
        ref = buf.at[pl.ds(1, NCTX - 1)]
        pltpu.make_async_copy(ref, ref, sem).wait()

    kv_wait(recv_k, kv_r.at[0])

    def second_part(i, carry):
        g, h = lax.div(i, HEADS), lax.rem(i, HEADS)
        rows = pl.ds(pl.multiple_of(g * BLOCK, BLOCK), BLOCK)
        cols = pl.ds(pl.multiple_of(h * DH, DH), DH)
        s = (
            lax.dot_general(
                q[rows, cols],
                chosen(recv_k, i),
                NT,
                preferred_element_type=jnp.float32,
            )
            * SCALE
        )
        m_old = top[i][:, :1]
        m = jnp.maximum(m_old, jnp.max(s, axis=1, keepdims=True))
        p = jnp.exp(s - m)
        shrink = jnp.exp(m_old - m)
        prob[i] = p.astype(jnp.bfloat16)
        acc[i] = acc[i] * shrink
        total = tot[i][:, :1] * shrink + jnp.sum(p, axis=1, keepdims=True)
        tot[i] = jnp.broadcast_to(total, (BLOCK, DH))
        return carry

    lax.fori_loop(0, GROUPS * HEADS, second_part, 0)
    kv_wait(recv_v, kv_r.at[1])

    def part(h, g):
        return att.at[h, pl.ds(g * BLOCK, BLOCK)]

    def att_copy(h, g, send, recv, to):
        return remote(part(h, g), part(h, g), send, recv, ctx, to)

    started = []

    def go(c):
        c.start()
        started.append(c)

    up_lane, dn_lane, far_lane = 2 * x_up + core, 2 * x_dn + core, 2 * x_far + core
    up_mate, dn_mate = 2 * x_up + 1 - core, 2 * x_dn + 1 - core
    far_mate = 2 * x_far + 1 - core
    for g in range(GROUPS):
        for h in range(HEADS):
            i = g * HEADS + h
            total = acc[i] + jnp.dot(
                prob[i], chosen(recv_v, i), preferred_element_type=jnp.float32
            )
            att[head, g * BLOCK : (g + 1) * BLOCK, h * DH : (h + 1) * DH] = (
                total / tot[i]
            ).astype(jnp.bfloat16)
        go(att_copy(head, g, xs_s.at[0, g], xs_r.at[0, g], up_lane))
        go(att_copy(head, g, xs_s.at[1, g], xs_r.at[1, g], dn_lane))
        go(att_copy(head, g, mate_s.at[g], mate_r.at[g], mate))

    def add(h, first=False):
        prod = lax.dot_general(
            att[h],
            w_all[pl.ds(h * 8, 8)].reshape(WIDTH, WIDTH),
            NT,
            preferred_element_type=jnp.float32,
        )
        if first:
            sums[...] = prod
        else:
            sums[...] += prod

    def forward(g, d):
        lane_of = dn_lane if d == 0 else up_lane
        att_copy(lane_of, g, xs_s.at[d, g], xs_r.at[d, g], mate).wait_recv()
        if (d == 0) == (g < GROUPS // 2):
            go(
                att_copy(
                    lane_of, g, far_s.at[g], far_r.at[g], up_lane if d == 0 else dn_lane
                )
            )
        go(att_copy(lane_of, g, fwd_s.at[d, g], fwd_r.at[d, g], mate))

    for g in range(GROUPS):
        for d in (0, 1):
            forward(g, d)
        if g == 0:
            add(head, first=True)
    for g in range(GROUPS):
        att_copy(mate, g, mate_s.at[g], mate_r.at[g], mate).wait_recv()
    for g in range(GROUPS):
        att_copy(far_lane, g, far_s.at[g], far_r.at[g], mate).wait_recv()
        go(att_copy(far_lane, g, ffw_s.at[g], ffw_r.at[g], mate))
    add(mate)
    add(dn_lane)
    add(up_lane)
    for d, h in ((0, dn_mate), (1, up_mate)):
        for g in range(GROUPS):
            att_copy(h, g, fwd_s.at[d, g], fwd_r.at[d, g], mate).wait_recv()
        add(h)
    add(far_lane)
    for g in range(GROUPS):
        att_copy(far_mate, g, ffw_s.at[g], ffw_r.at[g], mate).wait_recv()
    add(far_mate)
    out[...] = sums[...].astype(jnp.bfloat16)

    for c in started:
        c.wait_send()
    kv_wait(send_k, kv_s.at[0])
    kv_wait(send_v, kv_s.at[1])
    for c in y_first(w_all, yw_s, yw_r) + y_second(w_all, yw_s, yw_r):
        c.wait_send()
    for c in y_first(land_all, yl_s, yl_r) + y_second(land_all, yl_s, yl_r):
        c.wait_send()
    to_mate.wait_send()
    for s in range(STEPS):
        for d in (0, 1):
            if s < STEPS - d:
                land_ring(s, d, land_s, land_r).wait_send()
                w_ring(s, d, wz_s, wz_r).wait_send()
    rest = pick_all.at[pl.ds(1, NCTX - 1)]
    pltpu.make_async_copy(rest, rest, pick_sem.at[0]).wait()

    @pl.when(off_diag)
    def _():
        swap.wait_send()


def local(
    queries,
    span_keys,
    span_values,
    cache_keys,
    cache_values,
    land_keys,
    land_values,
    out_weight,
    selection,
):
    picks = selection.reshape(GROUPS * HEADS * PICKS)
    pick_row = jnp.broadcast_to(jnp.pad(picks, (0, 64))[None, :], (8, 128))
    land = jnp.concatenate([land_keys, land_values], axis=0)
    bf16, f32, i32 = jnp.bfloat16, jnp.float32, jnp.int32
    vmem = pl.BlockSpec(memory_space=pltpu.VMEM)
    dma = pltpu.SemaphoreType.DMA
    pairs = GROUPS * HEADS
    return pl.pallas_call(
        kernel,
        out_shape=jax.ShapeDtypeStruct((ROWS, WIDTH), bf16),
        in_specs=[pl.BlockSpec(memory_space=pltpu.SMEM)] + [vmem] * 8,
        out_specs=vmem,
        scratch_shapes=[
            pltpu.VMEM((NCTX, 8, 128), i32),
            pltpu.VMEM((NCTX, 128), i32),
            pltpu.SMEM((NCTX, 128), i32),
            pltpu.VMEM((NCTX, 2 * LAND, WIDTH), bf16),
            pltpu.VMEM((NZ, BLOCK, WIDTH), bf16),
            pltpu.VMEM((NCTX, BLOCK, WIDTH), bf16),
            pltpu.VMEM((NCTX, BLOCK, DH), bf16),
            pltpu.VMEM((NCTX, BLOCK, DH), bf16),
            pltpu.VMEM((NCTX, BLOCK, DH), bf16),
            pltpu.VMEM((NCTX, BLOCK, DH), bf16),
            pltpu.VMEM((8, ROWS, WIDTH), bf16),
            pltpu.VMEM((pairs, BLOCK, PICKS * BLOCK), bf16),
            pltpu.VMEM((pairs, BLOCK, DH), f32),
            pltpu.VMEM((pairs, BLOCK, DH), f32),
            pltpu.VMEM((pairs, BLOCK, DH), f32),
            pltpu.VMEM((ROWS, WIDTH), f32),
            pltpu.VMEM((BLOCKS * HEADS, BLOCK, DH), bf16),
            pltpu.VMEM((BLOCKS * HEADS, BLOCK, DH), bf16),
            dma((2,)),
            dma((1,)),
            dma((2, STEPS)),
            dma((2, STEPS)),
            dma((2,)),
            dma((2, STEPS)),
            dma((2, STEPS)),
            dma((3,)),
            dma((4,)),
            dma((4,)),
            dma((4,)),
            dma((4,)),
            dma((2,)),
            dma((2,)),
            dma((GROUPS,)),
            dma((GROUPS,)),
            dma((2, GROUPS)),
            dma((2, GROUPS)),
            dma((2, GROUPS)),
            dma((2, GROUPS)),
            dma((GROUPS,)),
            dma((GROUPS,)),
            dma((GROUPS,)),
            dma((GROUPS,)),
        ],
        compiler_params=pltpu.CompilerParams(
            collective_id=0, has_side_effects=True, vmem_limit_bytes=56 << 20
        ),
        name="landmark_attention",
    )(
        slots_of(picks),
        pick_row,
        queries,
        span_keys,
        span_values,
        cache_keys,
        cache_values,
        land,
        out_weight.T,
    )


def solution(mesh):
    in_specs = (P("ctx", "head"),) * 7 + (P("head", "ctx"), P("ctx", "head", None))
    return jax.shard_map(
        local, mesh=mesh, in_specs=in_specs, out_specs=P("ctx", "head"), check_vma=False
    )
```

```python
import functools
import math

import jax
import jax.numpy as jnp
from jax import lax
from jax.experimental import pallas as pl
from jax.experimental.pallas import tpu as pltpu
from jax.sharding import PartitionSpec as P

MESH = pl.DeviceIdType.MESH
BLOCK = 64
NY, NZ, NX = 4, 16, 4
NCTX = NY * NZ
GROUPS, HEADS, PICKS, DH = 4, 4, 4, 128
ROWS, WIDTH = GROUPS * BLOCK, HEADS * DH
LAND = 16
BLOCKS = 16
STEPS = NZ // 2
PER_STEP = 12
NT = (((1,), (1,)), ((), ()))
SCALE = 1.0 / math.sqrt(DH)


def offsets(i):
    k, dy = lax.div(i, 4), lax.rem(i, 4)
    odd = lax.rem(k, 2)
    dz = lax.rem(odd * lax.div(k + 1, 2) + (1 - odd) * (NZ - lax.div(k, 2)), NZ)
    return dy, dz


def slot_of(dy, dz):
    return NY * dz + dy


def remote(src, dst, send, recv, ctx, head):
    return pltpu.make_async_remote_copy(
        src_ref=src,
        dst_ref=dst,
        send_sem=send,
        recv_sem=recv,
        device_id=(ctx, head),
        device_id_type=MESH,
    )


def kernel(
    picks,
    q_in,
    sk_in,
    sv_in,
    ck_in,
    cv_in,
    lk_in,
    lv_in,
    wt,
    out,
    pick_row,
    pick_all,
    code_v,
    code_s,
    q,
    sk,
    sv,
    land_all,
    w_lane,
    w_all,
    send_k,
    send_v,
    recv_k,
    recv_v,
    att,
    prob,
    acc,
    top,
    tot,
    sums,
    pair_k,
    pair_v,
    pick_sem,
    code_sem,
    in_sem,
    land_s,
    land_r,
    swap_sem,
    wz_s,
    wz_r,
    core_sem,
    yl_s,
    yl_r,
    yw_s,
    yw_r,
    kv_s,
    kv_r,
    mate_s,
    mate_r,
    xs_s,
    xs_r,
    fwd_s,
    fwd_r,
    far_s,
    far_r,
    ffw_s,
    ffw_r,
):
    ctx, head = lax.axis_index("ctx"), lax.axis_index("head")
    y, z = lax.div(ctx, NZ), lax.rem(ctx, NZ)
    x, core = lax.div(head, 2), lax.rem(head, 2)
    mate = 2 * x + 1 - core
    x_up, x_dn = lax.rem(x + 1, NX), lax.rem(x + NX - 1, NX)
    x_far = lax.rem(x + 2, NX)
    z_up = y * NZ + lax.rem(z + 1, NZ)
    z_dn = y * NZ + lax.rem(z + NZ - 1, NZ)
    swap_ctx, swap_head = x * NZ + z, 2 * y + core
    off_diag = x != y

    def peer(i):
        dy, dz = offsets(i)
        return lax.rem(y + dy, NY) * NZ + lax.rem(z + dz, NZ)

    barrier = pltpu.get_barrier_semaphore()

    def greet(i, carry):
        pl.semaphore_signal(
            barrier, inc=1, device_id=(peer(i), head), device_id_type=MESH
        )
        return carry

    lax.fori_loop(1, NCTX, greet, 0)
    for h in (mate, 2 * x_up + core, 2 * x_dn + core):
        pl.semaphore_signal(barrier, inc=1, device_id=(ctx, h), device_id_type=MESH)
    for dy in range(1, NY):
        to = lax.rem(y + dy, NY) * NZ + z
        pl.semaphore_signal(barrier, inc=1, device_id=(to, mate), device_id_type=MESH)

    @pl.when(off_diag)
    def _():
        pl.semaphore_signal(
            barrier, inc=1, device_id=(swap_ctx, swap_head), device_id_type=MESH
        )

    loads = [
        pltpu.make_async_copy(src, dst, in_sem.at[n])
        for n, (src, dst) in enumerate(
            [
                (lk_in, land_all.at[ctx, pl.ds(0, LAND)]),
                (lv_in, land_all.at[ctx, pl.ds(LAND, LAND)]),
            ]
            + [
                (src.at[:, :, pl.ds(h * DH, DH)], dst.at[pl.ds(h * BLOCKS, BLOCKS)])
                for src, dst in ((ck_in, pair_k), (cv_in, pair_v))
                for h in range(HEADS)
            ]
            + [(q_in, q), (sk_in, sk), (sv_in, sv)]
        )
    ]
    for c in loads:
        c.start()
    own_w = pltpu.make_async_copy(wt, w_lane.at[z], swap_sem.at[2])

    @pl.when(x == y)
    def _():
        own_w.start()

    lane = lax.broadcasted_iota(jnp.int32, (1, 128), 1)
    row = jnp.zeros((1, 128), jnp.int32)
    for j in range(GROUPS * HEADS * PICKS):
        row = jnp.where(
            lane == j, picks[j // (HEADS * PICKS), j // PICKS % HEADS, j % PICKS], row
        )
    pick_row[...] = row
    for c in loads[:2]:
        c.wait()

    @pl.when(x == y)
    def _():
        own_w.wait()

    pl.semaphore_wait(barrier, NCTX - 1 + 3 + NY - 1 + jnp.where(off_diag, 1, 0))

    def ring(buf, base, s, d, send, recv):
        slot = base + lax.rem(z + (NZ - s if d == 0 else s), NZ)
        return remote(
            buf.at[slot],
            buf.at[slot],
            send.at[d, s],
            recv.at[d, s],
            z_up if d == 0 else z_dn,
            head,
        )

    def ring_in(buf, base, s, d, send, recv):
        slot = base + lax.rem(z + (NZ - s - 1 if d == 0 else s + 1), NZ)
        return remote(
            buf.at[slot],
            buf.at[slot],
            send.at[d, s],
            recv.at[d, s],
            z_up if d == 0 else z_dn,
            head,
        )

    land_ring = functools.partial(ring, land_all, y * NZ)
    land_in = functools.partial(ring_in, land_all, y * NZ)
    w_ring = functools.partial(ring, w_lane, 0)
    w_in = functools.partial(ring_in, w_lane, 0)
    def spread_land(zz):
        for dy in range(1, NY):
            ref = land_all.at[y * NZ + zz]
            to = lax.rem(y + dy, NY) * NZ + z
            remote(ref, ref, yl_s.at[dy], yl_r.at[dy], to, head).start()

    def spread_weights(zz):
        src = w_lane.at[zz]
        half_of = lax.div(zz, NZ // 2)
        dst = w_all.at[head_row * 8 + lax.rem(zz, NZ // 2)]
        taker = 2 * x + half_of
        for dy in range(1, NY):
            to = lax.rem(y + dy, NY) * NZ + z
            remote(src, dst, yw_s.at[dy], yw_r.at[dy], to, taker).start()

        @pl.when(half_of == core)
        def _():
            pltpu.make_async_copy(src, dst, core_sem.at[2]).start()

        @pl.when(half_of != core)
        def _():
            remote(src, dst, core_sem.at[0], core_sem.at[1], ctx, mate).start()

    head_row = 2 * y + core
    for d in (0, 1):
        land_ring(0, d, land_s, land_r).start()
    swap = remote(
        wt, w_lane.at[z], swap_sem.at[0], swap_sem.at[1], swap_ctx, swap_head
    )

    @pl.when(off_diag)
    def _():
        swap.start()

    own_picks = pltpu.make_async_copy(pick_row, pick_all.at[ctx], pick_sem.at[1])
    own_picks.start()

    def tell(i, carry):
        remote(
            pick_row,
            pick_all.at[ctx],
            pick_sem.at[0],
            pick_sem.at[1],
            peer(i),
            head,
        ).start()
        return carry

    lax.fori_loop(1, NCTX, tell, 0)

    @pl.when(off_diag)
    def _():
        swap.wait_recv()

    for d in (0, 1):
        w_ring(0, d, wz_s, wz_r).start()
    spread_land(z)
    spread_weights(z)
    pltpu.make_async_copy(pick_all, pick_all, pick_sem.at[1]).wait()
    asked = pick_all[:, 0, :]
    lane = lax.broadcasted_iota(jnp.int32, asked.shape, 1)
    mine = jnp.logical_and(lane < GROUPS * HEADS * PICKS, (asked >> 4) == ctx)
    code = jnp.where(mine, (asked & 15) + ((lane >> 2) & 3) * BLOCKS, 0)
    code = jnp.max(code, axis=1, keepdims=True)
    code_v[...] = jnp.broadcast_to(code, code_v.shape)
    to_scalar = pltpu.make_async_copy(code_v, code_s, code_sem.at[0])
    to_scalar.start()
    to_scalar.wait()

    def block_for(cache, t):
        return cache[code_s[t, 0]]

    for c in loads[2:]:
        c.wait()
    recv_k[0] = block_for(pair_k, ctx)
    recv_v[0] = block_for(pair_v, ctx)

    def send_block(cache, out_buf, in_buf, which, j, carry):
        t, i = peer(j), slot_of(*offsets(j))
        out_buf[i] = block_for(cache, t)
        remote(
            out_buf.at[i], in_buf.at[i], kv_s.at[which], kv_r.at[which], t, head
        ).start()
        return carry

    send_key = functools.partial(send_block, pair_k, send_k, recv_k, 0)
    send_value = functools.partial(send_block, pair_v, send_v, recv_v, 1)

    def send_blocks(first, last):
        cut = NCTX - 1
        if first < cut:
            lax.fori_loop(first + 1, min(last, cut) + 1, send_key, 0)
        if last > cut:
            lax.fori_loop(max(first, cut) - cut + 1, last - cut + 1, send_value, 0)

    for s in range(STEPS):
        for d in (0, 1):
            if d == 0 or s < STEPS - 1:
                land_in(s, d, land_s, land_r).wait_recv()
                nxt = s + 1
                if nxt < STEPS - d:
                    land_ring(nxt, d, land_s, land_r).start()
                w_in(s, d, wz_s, wz_r).wait_recv()
                if nxt < STEPS - d:
                    w_ring(nxt, d, wz_s, wz_r).start()
                zz = lax.rem(z + (NZ - nxt if d == 0 else nxt), NZ)
                spread_land(zz)
                spread_weights(zz)
        send_blocks(PER_STEP * s, PER_STEP * (s + 1))

    send_blocks(PER_STEP * STEPS, 2 * (NCTX - 1))

    def row_wait(buf, sem, row, n):
        ref = buf.at[pl.ds(row * n, n)]
        pltpu.make_async_copy(ref, ref, sem).wait()

    for dy in range(1, NY):
        row_wait(land_all, yl_r.at[dy], lax.rem(y + NY - dy, NY), NZ)

    def first_part(i, carry):
        g, h = lax.div(i, HEADS), lax.rem(i, HEADS)
        rows = pl.ds(pl.multiple_of(g * BLOCK, BLOCK), BLOCK)
        cols = pl.ds(pl.multiple_of(h * DH, DH), DH)
        qv = q[rows, cols]
        lk = land_all[:, 0:LAND, cols].reshape(NCTX * LAND, DH)
        lv = land_all[:, LAND : 2 * LAND, cols].reshape(NCTX * LAND, DH)
        s_l = lax.dot_general(qv, lk, NT, preferred_element_type=jnp.float32) * SCALE
        s_s = (
            lax.dot_general(
                qv, sk[rows, cols], NT, preferred_element_type=jnp.float32
            )
            * SCALE
        )
        causal = lax.broadcasted_iota(jnp.int32, s_s.shape, 0) >= lax.broadcasted_iota(
            jnp.int32, s_s.shape, 1
        )
        s_s = jnp.where(causal, s_s, -jnp.inf)
        m = jnp.maximum(
            jnp.max(s_l, axis=1, keepdims=True), jnp.max(s_s, axis=1, keepdims=True)
        )
        p_l, p_s = jnp.exp(s_l - m), jnp.exp(s_s - m)
        total = jnp.sum(p_l, axis=1, keepdims=True) + jnp.sum(
            p_s, axis=1, keepdims=True
        )
        acc[i] = jnp.dot(
            p_l.astype(jnp.bfloat16), lv, preferred_element_type=jnp.float32
        ) + jnp.dot(
            p_s.astype(jnp.bfloat16),
            sv[rows, cols],
            preferred_element_type=jnp.float32,
        )
        top[i] = jnp.broadcast_to(m, (BLOCK, DH))
        tot[i] = jnp.broadcast_to(total, (BLOCK, DH))
        return carry

    lax.fori_loop(0, GROUPS * HEADS, first_part, 0)


    def chosen(buf, i):
        blocks = []
        for p in range(PICKS):
            owner = picks[lax.div(i, HEADS), lax.rem(i, HEADS), p] >> 4
            slot = slot_of((y - (owner >> 4)) & 3, (z - (owner & 15)) & 15)
            blocks.append(buf[slot])
        return jnp.concatenate(blocks, axis=0)

    def kv_wait(buf, sem):
        ref = buf.at[pl.ds(1, NCTX - 1)]
        pltpu.make_async_copy(ref, ref, sem).wait()

    kv_wait(recv_k, kv_r.at[0])

    def second_part(i, carry):
        g, h = lax.div(i, HEADS), lax.rem(i, HEADS)
        rows = pl.ds(pl.multiple_of(g * BLOCK, BLOCK), BLOCK)
        cols = pl.ds(pl.multiple_of(h * DH, DH), DH)
        s = (
            lax.dot_general(
                q[rows, cols],
                chosen(recv_k, i),
                NT,
                preferred_element_type=jnp.float32,
            )
            * SCALE
        )
        m_old = top[i][:, :1]
        m = jnp.maximum(m_old, jnp.max(s, axis=1, keepdims=True))
        p = jnp.exp(s - m)
        shrink = jnp.exp(m_old - m)
        prob[i] = p.astype(jnp.bfloat16)
        acc[i] = acc[i] * shrink
        total = tot[i][:, :1] * shrink + jnp.sum(p, axis=1, keepdims=True)
        tot[i] = jnp.broadcast_to(total, (BLOCK, DH))
        return carry

    lax.fori_loop(0, GROUPS * HEADS, second_part, 0)
    for dy in range(1, NY):
        row_wait(w_all, yw_r.at[dy], lax.rem(y + NY - dy, NY), NZ)
    row_wait(w_all, core_sem.at[1], 2 * y + 1 - core, NZ // 2)
    row_wait(w_all, core_sem.at[2], 2 * y + core, NZ // 2)
    kv_wait(recv_v, kv_r.at[1])

    def att_copy(h, g, send, recv, to, half=None):
        rows = (
            pl.ds(g * BLOCK, BLOCK)
            if half is None
            else pl.ds(g * BLOCK + half * (BLOCK // 2), BLOCK // 2)
        )
        ref = att.at[h, rows]
        return remote(ref, ref, send, recv, ctx, to)

    started = []

    def go(c):
        c.start()
        started.append(c)

    up_lane, dn_lane, far_lane = 2 * x_up + core, 2 * x_dn + core, 2 * x_far + core
    up_mate, dn_mate = 2 * x_up + 1 - core, 2 * x_dn + 1 - core
    far_mate = 2 * x_far + 1 - core
    for g in range(GROUPS):
        for h in range(HEADS):
            i = g * HEADS + h
            total = acc[i] + jnp.dot(
                prob[i], chosen(recv_v, i), preferred_element_type=jnp.float32
            )
            att[head, g * BLOCK : (g + 1) * BLOCK, h * DH : (h + 1) * DH] = (
                total / tot[i]
            ).astype(jnp.bfloat16)
        go(att_copy(head, g, xs_s.at[0, g], xs_r.at[0, g], up_lane))
        go(att_copy(head, g, xs_s.at[1, g], xs_r.at[1, g], dn_lane))
        go(att_copy(head, g, mate_s.at[g], mate_r.at[g], mate))

    def add(h, first=False):
        prod = lax.dot_general(
            att[h],
            w_all[pl.ds(h * 8, 8)].reshape(WIDTH, WIDTH),
            NT,
            preferred_element_type=jnp.float32,
        )
        if first:
            sums[...] = prod
        else:
            sums[...] += prod

    def forward(g, d):
        lane_of = dn_lane if d == 0 else up_lane
        att_copy(lane_of, g, xs_s.at[d, g], xs_r.at[d, g], mate).wait_recv()
        to = up_lane if d == 0 else dn_lane
        go(att_copy(lane_of, g, far_s.at[d, g], far_r.at[d, g], to, half=d))
        go(att_copy(lane_of, g, fwd_s.at[d, g], fwd_r.at[d, g], mate))

    for g in range(GROUPS):
        for d in (0, 1):
            forward(g, d)
        if g == 0:
            add(head, first=True)
    for g in range(GROUPS):
        att_copy(mate, g, mate_s.at[g], mate_r.at[g], mate).wait_recv()
    for g in range(GROUPS):
        for d in (0, 1):
            att_copy(
                far_lane, g, far_s.at[d, g], far_r.at[d, g], mate, half=d
            ).wait_recv()
        go(att_copy(far_lane, g, ffw_s.at[g], ffw_r.at[g], mate))
    add(mate)
    add(dn_lane)
    add(up_lane)
    for d, h in ((0, dn_mate), (1, up_mate)):
        for g in range(GROUPS):
            att_copy(h, g, fwd_s.at[d, g], fwd_r.at[d, g], mate).wait_recv()
        add(h)
    add(far_lane)
    for g in range(GROUPS):
        att_copy(far_mate, g, ffw_s.at[g], ffw_r.at[g], mate).wait_recv()
    add(far_mate)
    out[...] = sums[...].astype(jnp.bfloat16)

    for c in started:
        c.wait_send()
    kv_wait(send_k, kv_s.at[0])
    kv_wait(send_v, kv_s.at[1])
    for dy in range(1, NY):
        row_wait(land_all, yl_s.at[dy], y, NZ)
        row_wait(w_lane, yw_s.at[dy], 0, NZ)
    row_wait(w_lane, core_sem.at[0], 1 - core, NZ // 2)
    for s in range(STEPS):
        for d in (0, 1):
            if s < STEPS - d:
                land_ring(s, d, land_s, land_r).wait_send()
                w_ring(s, d, wz_s, wz_r).wait_send()
    rest = pick_all.at[pl.ds(1, NCTX - 1)]
    pltpu.make_async_copy(rest, rest, pick_sem.at[0]).wait()

    @pl.when(off_diag)
    def _():
        swap.wait_send()


def local(
    queries,
    span_keys,
    span_values,
    cache_keys,
    cache_values,
    land_keys,
    land_values,
    out_weight,
    selection,
):
    bf16, f32, i32 = jnp.bfloat16, jnp.float32, jnp.int32
    vmem = pl.BlockSpec(memory_space=pltpu.VMEM)
    dma = pltpu.SemaphoreType.DMA
    pairs = GROUPS * HEADS
    return pl.pallas_call(
        kernel,
        out_shape=jax.ShapeDtypeStruct((ROWS, WIDTH), bf16),
        in_specs=[pl.BlockSpec(memory_space=pltpu.SMEM)]
        + [pl.BlockSpec(memory_space=pl.ANY)] * 8,
        out_specs=vmem,
        scratch_shapes=[
            pltpu.VMEM((1, 128), i32),
            pltpu.VMEM((NCTX, 1, 128), i32),
            pltpu.VMEM((NCTX, 128), i32),
            pltpu.SMEM((NCTX, 128), i32),
            pltpu.VMEM((ROWS, WIDTH), bf16),
            pltpu.VMEM((ROWS, WIDTH), bf16),
            pltpu.VMEM((ROWS, WIDTH), bf16),
            pltpu.VMEM((NCTX, 2 * LAND, WIDTH), bf16),
            pltpu.VMEM((NZ, BLOCK, WIDTH), bf16),
            pltpu.VMEM((NCTX, BLOCK, WIDTH), bf16),
            pltpu.VMEM((NCTX, BLOCK, DH), bf16),
            pltpu.VMEM((NCTX, BLOCK, DH), bf16),
            pltpu.VMEM((NCTX, BLOCK, DH), bf16),
            pltpu.VMEM((NCTX, BLOCK, DH), bf16),
            pltpu.VMEM((8, ROWS, WIDTH), bf16),
            pltpu.VMEM((pairs, BLOCK, PICKS * BLOCK), bf16),
            pltpu.VMEM((pairs, BLOCK, DH), f32),
            pltpu.VMEM((pairs, BLOCK, DH), f32),
            pltpu.VMEM((pairs, BLOCK, DH), f32),
            pltpu.VMEM((ROWS, WIDTH), f32),
            pltpu.VMEM((BLOCKS * HEADS, BLOCK, DH), bf16),
            pltpu.VMEM((BLOCKS * HEADS, BLOCK, DH), bf16),
            dma((2,)),
            dma((1,)),
            dma((13,)),
            dma((2, STEPS)),
            dma((2, STEPS)),
            dma((3,)),
            dma((2, STEPS)),
            dma((2, STEPS)),
            dma((3,)),
            dma((4,)),
            dma((4,)),
            dma((4,)),
            dma((4,)),
            dma((2,)),
            dma((2,)),
            dma((GROUPS,)),
            dma((GROUPS,)),
            dma((2, GROUPS)),
            dma((2, GROUPS)),
            dma((2, GROUPS)),
            dma((2, GROUPS)),
            dma((2, GROUPS)),
            dma((2, GROUPS)),
            dma((GROUPS,)),
            dma((GROUPS,)),
        ],
        compiler_params=pltpu.CompilerParams(
            collective_id=0, has_side_effects=True, vmem_limit_bytes=56 << 20
        ),
        name="landmark_attention",
    )(
        selection,
        queries,
        span_keys,
        span_values,
        cache_keys.reshape(BLOCKS, BLOCK, WIDTH),
        cache_values.reshape(BLOCKS, BLOCK, WIDTH),
        land_keys,
        land_values,
        out_weight.T,
    )


def solution(mesh):
    in_specs = (P("ctx", "head"),) * 7 + (P("head", "ctx"), P("ctx", "head", None))
    return jax.shard_map(
        local, mesh=mesh, in_specs=in_specs, out_specs=P("ctx", "head"), check_vma=False
    )
```

```python
import functools
import math

import jax
import jax.numpy as jnp
from jax import lax
from jax.experimental import pallas as pl
from jax.experimental.pallas import tpu as pltpu
from jax.sharding import PartitionSpec as P

MESH = pl.DeviceIdType.MESH
BLOCK = 64
NY, NZ, NX = 4, 16, 4
NCTX = NY * NZ
GROUPS, HEADS, PICKS, DH = 4, 4, 4, 128
ROWS, WIDTH = GROUPS * BLOCK, HEADS * DH
LAND = 16
BLOCKS = 16
STEPS = NZ // 2
EXTRA = 32
LANE_ROWS = (BLOCK - EXTRA, BLOCK + EXTRA)
PER_STEP = 12
NT = (((1,), (1,)), ((), ()))
SCALE = 1.0 / math.sqrt(DH)


def offsets(i):
    k, dy = lax.div(i, 4), lax.rem(i, 4)
    odd = lax.rem(k, 2)
    dz = lax.rem(odd * lax.div(k + 1, 2) + (1 - odd) * (NZ - lax.div(k, 2)), NZ)
    return dy, dz


def slot_of(dy, dz):
    return NY * dz + dy


def remote(src, dst, send, recv, ctx, head):
    return pltpu.make_async_remote_copy(
        src_ref=src,
        dst_ref=dst,
        send_sem=send,
        recv_sem=recv,
        device_id=(ctx, head),
        device_id_type=MESH,
    )


def kernel(
    picks,
    q_in,
    sk_in,
    sv_in,
    ck_in,
    cv_in,
    lk_in,
    lv_in,
    wt,
    out,
    pick_row,
    pick_all,
    code_v,
    code_s,
    q,
    sk,
    sv,
    land_all,
    w_lane0,
    w_lane1,
    w_all,
    send_k,
    send_v,
    recv_k,
    recv_v,
    att,
    prob,
    acc,
    top,
    tot,
    sums,
    pair_k,
    pair_v,
    pick_sem,
    code_sem,
    in_sem,
    land_s,
    land_r,
    swap_sem,
    wz_s,
    wz_r,
    core_sem,
    yl_s,
    yl_r,
    yw_s,
    yw_r,
    kv_s,
    kv_r,
    mate_s,
    mate_r,
    xs_s,
    xs_r,
    fwd_s,
    fwd_r,
    far_s,
    far_r,
    ffw_s,
    ffw_r,
):
    ctx, head = lax.axis_index("ctx"), lax.axis_index("head")
    y, z = lax.div(ctx, NZ), lax.rem(ctx, NZ)
    x, core = lax.div(head, 2), lax.rem(head, 2)
    mate = 2 * x + 1 - core
    x_up, x_dn = lax.rem(x + 1, NX), lax.rem(x + NX - 1, NX)
    x_far = lax.rem(x + 2, NX)
    z_up = y * NZ + lax.rem(z + 1, NZ)
    z_dn = y * NZ + lax.rem(z + NZ - 1, NZ)
    swap_ctx, swap_head = x * NZ + z, 2 * y
    off_diag = x != y

    def on_lane(f):
        for lane in (0, 1):
            pl.when(core == lane)(functools.partial(f, lane))

    def peer(i):
        dy, dz = offsets(i)
        return lax.rem(y + dy, NY) * NZ + lax.rem(z + dz, NZ)

    barrier = pltpu.get_barrier_semaphore()

    def greet(i, carry):
        pl.semaphore_signal(
            barrier, inc=1, device_id=(peer(i), head), device_id_type=MESH
        )
        return carry

    lax.fori_loop(1, NCTX, greet, 0, unroll=True)
    for h in (mate, 2 * x_up + core, 2 * x_dn + core):
        pl.semaphore_signal(barrier, inc=1, device_id=(ctx, h), device_id_type=MESH)
    for dy in range(1, NY):
        to = lax.rem(y + dy, NY) * NZ + z
        pl.semaphore_signal(barrier, inc=1, device_id=(to, mate), device_id_type=MESH)

    @pl.when(off_diag)
    def _():
        @on_lane
        def _(lane):
            for c in range(lane + 1):
                pl.semaphore_signal(
                    barrier,
                    inc=1,
                    device_id=(swap_ctx, swap_head + c),
                    device_id_type=MESH,
                )


    loads = [
        pltpu.make_async_copy(src, dst, in_sem.at[n])
        for n, (src, dst) in enumerate(
            [
                (lk_in, land_all.at[ctx, pl.ds(0, LAND)]),
                (lv_in, land_all.at[ctx, pl.ds(LAND, LAND)]),
            ]
            + [
                (src.at[:, :, pl.ds(h * DH, DH)], dst.at[pl.ds(h * BLOCKS, BLOCKS)])
                for src, dst in ((ck_in, pair_k), (cv_in, pair_v))
                for h in range(HEADS)
            ]
            + [(q_in, q), (sk_in, sk), (sv_in, sv)]
        )
    ]
    for c in loads:
        c.start()
    lanes = (w_lane0, w_lane1)
    kept = (wt.at[pl.ds(EXTRA, BLOCK - EXTRA)], wt)
    lent = wt.at[pl.ds(0, EXTRA)]
    place = (w_lane0.at[z], w_lane1.at[z, pl.ds(0, BLOCK)])
    lent_place = w_lane1.at[z, pl.ds(BLOCK, EXTRA)]

    def own_w(lane):
        return pltpu.make_async_copy(kept[lane], place[lane], swap_sem.at[2])

    def swap_main(lane):
        return remote(
            kept[lane],
            place[lane],
            swap_sem.at[0],
            swap_sem.at[2],
            swap_ctx,
            swap_head + lane,
        )

    swap_lent = remote(
        lent, lent_place, swap_sem.at[1], swap_sem.at[3], swap_ctx, swap_head + 1
    )

    @pl.when(x == y)
    def _():
        on_lane(lambda lane: own_w(lane).start())


    lane = lax.broadcasted_iota(jnp.int32, (1, 128), 1)
    row = jnp.zeros((1, 128), jnp.int32)
    for j in range(GROUPS * HEADS * PICKS):
        row = jnp.where(
            lane == j, picks[j // (HEADS * PICKS), j // PICKS % HEADS, j % PICKS], row
        )
    pick_row[...] = row
    for c in loads[:2]:
        c.wait()

    @pl.when(x == y)
    def _():
        on_lane(lambda lane: own_w(lane).wait())

    pl.semaphore_wait(barrier, NCTX - 1 + 3 + NY - 1 + jnp.where(off_diag, 2 - core, 0))

    def ring(buf, base, s, d, send, recv):
        slot = base + lax.rem(z + (NZ - s if d == 0 else s), NZ)
        return remote(
            buf.at[slot],
            buf.at[slot],
            send.at[d, s],
            recv.at[d, s],
            z_up if d == 0 else z_dn,
            head,
        )

    def ring_in(buf, base, s, d, send, recv):
        slot = base + lax.rem(z + (NZ - s - 1 if d == 0 else s + 1), NZ)
        return remote(
            buf.at[slot],
            buf.at[slot],
            send.at[d, s],
            recv.at[d, s],
            z_up if d == 0 else z_dn,
            head,
        )

    land_ring = functools.partial(ring, land_all, y * NZ)
    land_in = functools.partial(ring_in, land_all, y * NZ)
    w_ring = [functools.partial(ring, b, 0) for b in lanes]
    w_in = [functools.partial(ring_in, b, 0) for b in lanes]
    def spread_land(zz):
        for dy in range(1, NY):
            ref = land_all.at[y * NZ + zz]
            to = lax.rem(y + dy, NY) * NZ + z
            remote(ref, ref, yl_s.at[dy], yl_r.at[dy], to, head).start()

    def lane_rows(lane):
        return pl.ds(0, LANE_ROWS[1]) if lane else pl.ds(LANE_ROWS[1], LANE_ROWS[0])

    def spread_weights(lane, zz):
        src = lanes[lane].at[zz]
        half_of = lax.div(zz, NZ // 2)
        dst = w_all.at[y, lax.rem(zz, NZ // 2), lane_rows(lane)]
        taker = 2 * x + half_of
        for dy in range(1, NY):
            to = lax.rem(y + dy, NY) * NZ + z
            remote(src, dst, yw_s.at[dy], yw_r.at[lane, dy], to, taker).start()

        @pl.when(half_of == lane)
        def _():
            pltpu.make_async_copy(src, dst, core_sem.at[2]).start()

        @pl.when(half_of != lane)
        def _():
            remote(src, dst, core_sem.at[0], core_sem.at[1], ctx, mate).start()

    for d in (0, 1):
        land_ring(0, d, land_s, land_r).start()
    @pl.when(off_diag)
    def _():
        on_lane(lambda lane: swap_main(lane).start())

    @pl.when(core == 0)
    def _():
        swap_lent.start()

    own_picks = pltpu.make_async_copy(pick_row, pick_all.at[ctx], pick_sem.at[1])
    own_picks.start()

    def tell(i, carry):
        remote(
            pick_row,
            pick_all.at[ctx],
            pick_sem.at[0],
            pick_sem.at[1],
            peer(i),
            head,
        ).start()
        return carry

    lax.fori_loop(1, NCTX, tell, 0, unroll=True)

    spread_land(z)

    @pl.when(off_diag)
    def _():
        on_lane(lambda lane: swap_main(lane).wait_recv())

    @pl.when(core == 1)
    def _():
        swap_lent.wait_recv()

    @on_lane
    def _(lane):
        for d in (0, 1):
            w_ring[lane](0, d, wz_s, wz_r).start()
        spread_weights(lane, z)

    pltpu.make_async_copy(pick_all, pick_all, pick_sem.at[1]).wait()
    asked = pick_all[:, 0, :]
    lane = lax.broadcasted_iota(jnp.int32, asked.shape, 1)
    mine = jnp.logical_and(lane < GROUPS * HEADS * PICKS, (asked >> 4) == ctx)
    code = jnp.where(mine, (asked & 15) + ((lane >> 2) & 3) * BLOCKS, 0)
    code = jnp.max(code, axis=1, keepdims=True)
    code_v[...] = jnp.broadcast_to(code, code_v.shape)
    to_scalar = pltpu.make_async_copy(code_v, code_s, code_sem.at[0])
    to_scalar.start()
    to_scalar.wait()

    def block_for(cache, t):
        return cache[code_s[t, 0]]

    for c in loads[2:]:
        c.wait()
    recv_k[0] = block_for(pair_k, ctx)
    recv_v[0] = block_for(pair_v, ctx)

    def send_block(cache, out_buf, in_buf, which, j, carry):
        t, i = peer(j), slot_of(*offsets(j))
        out_buf[i] = block_for(cache, t)
        remote(
            out_buf.at[i], in_buf.at[i], kv_s.at[which], kv_r.at[which], t, head
        ).start()
        return carry

    send_key = functools.partial(send_block, pair_k, send_k, recv_k, 0)
    send_value = functools.partial(send_block, pair_v, send_v, recv_v, 1)

    def send_blocks(first, last):
        cut = NCTX - 1
        if first < cut:
            lax.fori_loop(first + 1, min(last, cut) + 1, send_key, 0)
        if last > cut:
            lax.fori_loop(max(first, cut) - cut + 1, last - cut + 1, send_value, 0)

    for s in range(STEPS):
        for d in (0, 1):
            if d == 0 or s < STEPS - 1:
                land_in(s, d, land_s, land_r).wait_recv()
                nxt = s + 1
                if nxt < STEPS - d:
                    land_ring(nxt, d, land_s, land_r).start()
                zz = lax.rem(z + (NZ - nxt if d == 0 else nxt), NZ)
                spread_land(zz)

                @on_lane
                def _(lane):
                    w_in[lane](s, d, wz_s, wz_r).wait_recv()
                    if nxt < STEPS - d:
                        w_ring[lane](nxt, d, wz_s, wz_r).start()
                    spread_weights(lane, zz)

        send_blocks(PER_STEP * s, PER_STEP * (s + 1))

    send_blocks(PER_STEP * STEPS, 2 * (NCTX - 1))

    def row_wait(buf, sem, row, n):
        ref = buf.at[pl.ds(row * n, n)]
        pltpu.make_async_copy(ref, ref, sem).wait()

    for dy in range(1, NY):
        row_wait(land_all, yl_r.at[dy], lax.rem(y + NY - dy, NY), NZ)

    def first_part(i, carry):
        g, h = lax.div(i, HEADS), lax.rem(i, HEADS)
        rows = pl.ds(pl.multiple_of(g * BLOCK, BLOCK), BLOCK)
        cols = pl.ds(pl.multiple_of(h * DH, DH), DH)
        qv = q[rows, cols]
        lk = land_all[:, 0:LAND, cols].reshape(NCTX * LAND, DH)
        lv = land_all[:, LAND : 2 * LAND, cols].reshape(NCTX * LAND, DH)
        s_l = lax.dot_general(qv, lk, NT, preferred_element_type=jnp.float32) * SCALE
        s_s = (
            lax.dot_general(
                qv, sk[rows, cols], NT, preferred_element_type=jnp.float32
            )
            * SCALE
        )
        causal = lax.broadcasted_iota(jnp.int32, s_s.shape, 0) >= lax.broadcasted_iota(
            jnp.int32, s_s.shape, 1
        )
        s_s = jnp.where(causal, s_s, -jnp.inf)
        m = jnp.maximum(
            jnp.max(s_l, axis=1, keepdims=True), jnp.max(s_s, axis=1, keepdims=True)
        )
        p_l, p_s = jnp.exp(s_l - m), jnp.exp(s_s - m)
        total = jnp.sum(p_l, axis=1, keepdims=True) + jnp.sum(
            p_s, axis=1, keepdims=True
        )
        acc[i] = jnp.dot(
            p_l.astype(jnp.bfloat16), lv, preferred_element_type=jnp.float32
        ) + jnp.dot(
            p_s.astype(jnp.bfloat16),
            sv[rows, cols],
            preferred_element_type=jnp.float32,
        )
        top[i] = jnp.broadcast_to(m, (BLOCK, DH))
        tot[i] = jnp.broadcast_to(total, (BLOCK, DH))
        return carry

    lax.fori_loop(0, GROUPS * HEADS, first_part, 0)


    def chosen(buf, i):
        blocks = []
        for p in range(PICKS):
            owner = picks[lax.div(i, HEADS), lax.rem(i, HEADS), p] >> 4
            slot = slot_of((y - (owner >> 4)) & 3, (z - (owner & 15)) & 15)
            blocks.append(buf[slot])
        return jnp.concatenate(blocks, axis=0)

    def kv_wait(buf, sem):
        ref = buf.at[pl.ds(1, NCTX - 1)]
        pltpu.make_async_copy(ref, ref, sem).wait()

    kv_wait(recv_k, kv_r.at[0])

    def second_part(i, carry):
        g, h = lax.div(i, HEADS), lax.rem(i, HEADS)
        rows = pl.ds(pl.multiple_of(g * BLOCK, BLOCK), BLOCK)
        cols = pl.ds(pl.multiple_of(h * DH, DH), DH)
        s = (
            lax.dot_general(
                q[rows, cols],
                chosen(recv_k, i),
                NT,
                preferred_element_type=jnp.float32,
            )
            * SCALE
        )
        m_old = top[i][:, :1]
        m = jnp.maximum(m_old, jnp.max(s, axis=1, keepdims=True))
        p = jnp.exp(s - m)
        shrink = jnp.exp(m_old - m)
        prob[i] = p.astype(jnp.bfloat16)
        acc[i] = acc[i] * shrink
        total = tot[i][:, :1] * shrink + jnp.sum(p, axis=1, keepdims=True)
        tot[i] = jnp.broadcast_to(total, (BLOCK, DH))
        return carry

    lax.fori_loop(0, GROUPS * HEADS, second_part, 0)
    def bytes_wait(ref, sem):
        pltpu.make_async_copy(ref, ref, sem).wait()

    for dy in range(1, NY):
        for lane in (0, 1):
            bytes_wait(
                w_all.at[lax.rem(y + NY - dy, NY), :, lane_rows(lane)],
                yw_r.at[lane, dy],
            )

    @on_lane
    def _(lane):
        bytes_wait(w_all.at[y, :, lane_rows(lane)], core_sem.at[2])
        bytes_wait(w_all.at[y, :, lane_rows(1 - lane)], core_sem.at[1])

    kv_wait(recv_v, kv_r.at[1])

    def att_copy(h, g, send, recv, to, half=None):
        rows = (
            pl.ds(g * BLOCK, BLOCK)
            if half is None
            else pl.ds(g * BLOCK + half * (BLOCK // 2), BLOCK // 2)
        )
        ref = att.at[h, rows]
        return remote(ref, ref, send, recv, ctx, to)

    started = []

    def go(c):
        c.start()
        started.append(c)

    up_lane, dn_lane, far_lane = 2 * x_up + core, 2 * x_dn + core, 2 * x_far + core
    up_mate, dn_mate = 2 * x_up + 1 - core, 2 * x_dn + 1 - core
    far_mate = 2 * x_far + 1 - core
    for g in range(GROUPS):
        for h in range(HEADS):
            i = g * HEADS + h
            total = acc[i] + jnp.dot(
                prob[i], chosen(recv_v, i), preferred_element_type=jnp.float32
            )
            att[head, g * BLOCK : (g + 1) * BLOCK, h * DH : (h + 1) * DH] = (
                total / tot[i]
            ).astype(jnp.bfloat16)
        go(att_copy(head, g, xs_s.at[0, g], xs_r.at[0, g], up_lane))
        go(att_copy(head, g, xs_s.at[1, g], xs_r.at[1, g], dn_lane))
        go(att_copy(head, g, mate_s.at[g], mate_r.at[g], mate))

    def add(h, first=False):
        prod = lax.dot_general(
            att[h],
            w_all[
                lax.div(h, 2),
                :,
                pl.ds(pl.multiple_of((1 - lax.rem(h, 2)) * BLOCK, BLOCK), BLOCK),
            ].reshape(WIDTH, WIDTH),
            NT,
            preferred_element_type=jnp.float32,
        )
        if first:
            sums[...] = prod
        else:
            sums[...] += prod

    def forward(g, d):
        lane_of = dn_lane if d == 0 else up_lane
        att_copy(lane_of, g, xs_s.at[d, g], xs_r.at[d, g], mate).wait_recv()
        to = up_lane if d == 0 else dn_lane
        go(att_copy(lane_of, g, far_s.at[d, g], far_r.at[d, g], to, half=d))
        go(att_copy(lane_of, g, fwd_s.at[d, g], fwd_r.at[d, g], mate))

    for g in range(GROUPS):
        for d in (0, 1):
            forward(g, d)
        if g == 0:
            add(head, first=True)
    for g in range(GROUPS):
        att_copy(mate, g, mate_s.at[g], mate_r.at[g], mate).wait_recv()
    for g in range(GROUPS):
        for d in (0, 1):
            att_copy(
                far_lane, g, far_s.at[d, g], far_r.at[d, g], mate, half=d
            ).wait_recv()
        go(att_copy(far_lane, g, ffw_s.at[g], ffw_r.at[g], mate))
    add(mate)
    add(dn_lane)
    add(up_lane)
    for d, h in ((0, dn_mate), (1, up_mate)):
        for g in range(GROUPS):
            att_copy(h, g, fwd_s.at[d, g], fwd_r.at[d, g], mate).wait_recv()
        add(h)
    add(far_lane)
    for g in range(GROUPS):
        att_copy(far_mate, g, ffw_s.at[g], ffw_r.at[g], mate).wait_recv()
    add(far_mate)
    out[...] = sums[...].astype(jnp.bfloat16)

    for c in started:
        c.wait_send()
    kv_wait(send_k, kv_s.at[0])
    kv_wait(send_v, kv_s.at[1])
    for dy in range(1, NY):
        row_wait(land_all, yl_s.at[dy], y, NZ)

    @on_lane
    def _(lane):
        for dy in range(1, NY):
            bytes_wait(lanes[lane], yw_s.at[dy])
        bytes_wait(lanes[lane].at[pl.ds(0, NZ // 2)], core_sem.at[0])

    for s in range(STEPS):
        for d in (0, 1):
            if s < STEPS - d:
                land_ring(s, d, land_s, land_r).wait_send()

    @on_lane
    def _(lane):
        for s in range(STEPS):
            for d in (0, 1):
                if s < STEPS - d:
                    w_ring[lane](s, d, wz_s, wz_r).wait_send()

    rest = pick_all.at[pl.ds(1, NCTX - 1)]
    pltpu.make_async_copy(rest, rest, pick_sem.at[0]).wait()

    @pl.when(off_diag)
    def _():
        on_lane(lambda lane: swap_main(lane).wait_send())

    @pl.when(core == 0)
    def _():
        swap_lent.wait_send()


def local(
    queries,
    span_keys,
    span_values,
    cache_keys,
    cache_values,
    land_keys,
    land_values,
    out_weight,
    selection,
):
    bf16, f32, i32 = jnp.bfloat16, jnp.float32, jnp.int32
    vmem = pl.BlockSpec(memory_space=pltpu.VMEM)
    dma = pltpu.SemaphoreType.DMA
    pairs = GROUPS * HEADS
    return pl.pallas_call(
        kernel,
        out_shape=jax.ShapeDtypeStruct((ROWS, WIDTH), bf16),
        in_specs=[pl.BlockSpec(memory_space=pltpu.SMEM)]
        + [pl.BlockSpec(memory_space=pl.ANY)] * 8,
        out_specs=vmem,
        scratch_shapes=[
            pltpu.VMEM((1, 128), i32),
            pltpu.VMEM((NCTX, 1, 128), i32),
            pltpu.VMEM((NCTX, 128), i32),
            pltpu.SMEM((NCTX, 128), i32),
            pltpu.VMEM((ROWS, WIDTH), bf16),
            pltpu.VMEM((ROWS, WIDTH), bf16),
            pltpu.VMEM((ROWS, WIDTH), bf16),
            pltpu.VMEM((NCTX, 2 * LAND, WIDTH), bf16),
            pltpu.VMEM((NZ, LANE_ROWS[0], WIDTH), bf16),
            pltpu.VMEM((NZ, LANE_ROWS[1], WIDTH), bf16),
            pltpu.VMEM((NY, NZ // 2, 2 * BLOCK, WIDTH), bf16),
            pltpu.VMEM((NCTX, BLOCK, DH), bf16),
            pltpu.VMEM((NCTX, BLOCK, DH), bf16),
            pltpu.VMEM((NCTX, BLOCK, DH), bf16),
            pltpu.VMEM((NCTX, BLOCK, DH), bf16),
            pltpu.VMEM((8, ROWS, WIDTH), bf16),
            pltpu.VMEM((pairs, BLOCK, PICKS * BLOCK), bf16),
            pltpu.VMEM((pairs, BLOCK, DH), f32),
            pltpu.VMEM((pairs, BLOCK, DH), f32),
            pltpu.VMEM((pairs, BLOCK, DH), f32),
            pltpu.VMEM((ROWS, WIDTH), f32),
            pltpu.VMEM((BLOCKS * HEADS, BLOCK, DH), bf16),
            pltpu.VMEM((BLOCKS * HEADS, BLOCK, DH), bf16),
            dma((2,)),
            dma((1,)),
            dma((13,)),
            dma((2, STEPS)),
            dma((2, STEPS)),
            dma((4,)),
            dma((2, STEPS)),
            dma((2, STEPS)),
            dma((3,)),
            dma((4,)),
            dma((4,)),
            dma((4,)),
            dma((2, 4)),
            dma((2,)),
            dma((2,)),
            dma((GROUPS,)),
            dma((GROUPS,)),
            dma((2, GROUPS)),
            dma((2, GROUPS)),
            dma((2, GROUPS)),
            dma((2, GROUPS)),
            dma((2, GROUPS)),
            dma((2, GROUPS)),
            dma((GROUPS,)),
            dma((GROUPS,)),
        ],
        compiler_params=pltpu.CompilerParams(
            collective_id=0, has_side_effects=True, vmem_limit_bytes=56 << 20
        ),
        name="landmark_attention",
    )(
        selection,
        queries,
        span_keys,
        span_values,
        cache_keys.reshape(BLOCKS, BLOCK, WIDTH),
        cache_values.reshape(BLOCKS, BLOCK, WIDTH),
        land_keys,
        land_values,
        out_weight.T,
    )


def solution(mesh):
    in_specs = (P("ctx", "head"),) * 7 + (P("head", "ctx"), P("ctx", "head", None))
    return jax.shard_map(
        local, mesh=mesh, in_specs=in_specs, out_specs=P("ctx", "head"), check_vma=False
    )
```

```python
import functools
import math

import jax
import jax.numpy as jnp
from jax import lax
from jax.experimental import pallas as pl
from jax.experimental.pallas import tpu as pltpu
from jax.sharding import PartitionSpec as P

MESH = pl.DeviceIdType.MESH
BLOCK = 64
NY, NZ, NX = 4, 16, 4
NCTX = NY * NZ
GROUPS, HEADS, PICKS, DH = 4, 4, 4, 128
ROWS, WIDTH = GROUPS * BLOCK, HEADS * DH
LAND = 16
BLOCKS = 16
STEPS = NZ // 2
EXTRA = 32
LANE_ROWS = (BLOCK - EXTRA, BLOCK + EXTRA)
PER_STEP = 12
NT = (((1,), (1,)), ((), ()))
SCALE = 1.0 / math.sqrt(DH)


def offsets(i):
    k, dy = lax.div(i, 4), lax.rem(i, 4)
    odd = lax.rem(k, 2)
    dz = lax.rem(odd * lax.div(k + 1, 2) + (1 - odd) * (NZ - lax.div(k, 2)), NZ)
    return dy, dz


def slot_of(dy, dz):
    return NY * dz + dy


def remote(src, dst, send, recv, ctx, head):
    return pltpu.make_async_remote_copy(
        src_ref=src,
        dst_ref=dst,
        send_sem=send,
        recv_sem=recv,
        device_id=(ctx, head),
        device_id_type=MESH,
    )


def kernel(
    picks,
    q_in,
    sk_in,
    sv_in,
    ck_in,
    cv_in,
    lk_in,
    lv_in,
    wt,
    out,
    pick_row,
    pick_all,
    code_v,
    code_s,
    q,
    sk,
    sv,
    land_all,
    w_lane0,
    w_lane1,
    w_all,
    send_k,
    send_v,
    recv_k,
    recv_v,
    att,
    prob,
    acc,
    top,
    tot,
    sums,
    pair_k,
    pair_v,
    pick_sem,
    code_sem,
    in_sem,
    land_s,
    land_r,
    swap_sem,
    wz_s,
    wz_r,
    core_sem,
    yl_s,
    yl_r,
    yw_s,
    yw_r,
    kv_s,
    kv_r,
    mate_s,
    mate_r,
    xs_s,
    xs_r,
    fwd_s,
    fwd_r,
    far_s,
    far_r,
    ffw_s,
    ffw_r,
):
    ctx, head = lax.axis_index("ctx"), lax.axis_index("head")
    y, z = lax.div(ctx, NZ), lax.rem(ctx, NZ)
    x, core = lax.div(head, 2), lax.rem(head, 2)
    mate = 2 * x + 1 - core
    x_up, x_dn = lax.rem(x + 1, NX), lax.rem(x + NX - 1, NX)
    x_far = lax.rem(x + 2, NX)
    z_up = y * NZ + lax.rem(z + 1, NZ)
    z_dn = y * NZ + lax.rem(z + NZ - 1, NZ)
    swap_ctx, swap_head = x * NZ + z, 2 * y
    off_diag = x != y

    def on_lane(f):
        for lane in (0, 1):
            pl.when(core == lane)(functools.partial(f, lane))

    def peer(i):
        dy, dz = offsets(i)
        return lax.rem(y + dy, NY) * NZ + lax.rem(z + dz, NZ)

    barrier = pltpu.get_barrier_semaphore()

    def greet(i, carry):
        pl.semaphore_signal(
            barrier, inc=1, device_id=(peer(NCTX - i), head), device_id_type=MESH
        )
        return carry

    lax.fori_loop(1, NCTX, greet, 0, unroll=True)
    for h in (mate, 2 * x_up + core, 2 * x_dn + core):
        pl.semaphore_signal(barrier, inc=1, device_id=(ctx, h), device_id_type=MESH)
    for dy in range(1, NY):
        to = lax.rem(y + dy, NY) * NZ + z
        pl.semaphore_signal(barrier, inc=1, device_id=(to, mate), device_id_type=MESH)

    @pl.when(off_diag)
    def _():
        @on_lane
        def _(lane):
            for c in range(lane + 1):
                pl.semaphore_signal(
                    barrier,
                    inc=1,
                    device_id=(swap_ctx, swap_head + c),
                    device_id_type=MESH,
                )


    loads = [
        pltpu.make_async_copy(src, dst, in_sem.at[n])
        for n, (src, dst) in enumerate(
            [
                (lk_in, land_all.at[ctx, pl.ds(0, LAND)]),
                (lv_in, land_all.at[ctx, pl.ds(LAND, LAND)]),
            ]
            + [
                (src.at[:, :, pl.ds(h * DH, DH)], dst.at[pl.ds(h * BLOCKS, BLOCKS)])
                for src, dst in ((ck_in, pair_k), (cv_in, pair_v))
                for h in range(HEADS)
            ]
            + [(q_in, q), (sk_in, sk), (sv_in, sv)]
        )
    ]
    for c in loads:
        c.start()
    lanes = (w_lane0, w_lane1)
    kept = (wt.at[pl.ds(EXTRA, BLOCK - EXTRA)], wt)
    lent = wt.at[pl.ds(0, EXTRA)]
    place = (w_lane0.at[z], w_lane1.at[z, pl.ds(0, BLOCK)])
    lent_place = w_lane1.at[z, pl.ds(BLOCK, EXTRA)]

    def own_w(lane):
        return pltpu.make_async_copy(kept[lane], place[lane], swap_sem.at[2])

    def swap_main(lane):
        return remote(
            kept[lane],
            place[lane],
            swap_sem.at[0],
            swap_sem.at[2],
            swap_ctx,
            swap_head + lane,
        )

    swap_lent = remote(
        lent, lent_place, swap_sem.at[1], swap_sem.at[3], swap_ctx, swap_head + 1
    )

    @pl.when(x == y)
    def _():
        on_lane(lambda lane: own_w(lane).start())


    lane = lax.broadcasted_iota(jnp.int32, (1, 128), 1)
    row = jnp.zeros((1, 128), jnp.int32)
    for j in range(GROUPS * HEADS * PICKS):
        row = jnp.where(
            lane == j, picks[j // (HEADS * PICKS), j // PICKS % HEADS, j % PICKS], row
        )
    pick_row[...] = row
    for c in loads[:2]:
        c.wait()

    @pl.when(x == y)
    def _():
        on_lane(lambda lane: own_w(lane).wait())

    pl.semaphore_wait(barrier, NCTX - 1 + 3 + NY - 1 + jnp.where(off_diag, 2 - core, 0))

    def ring(buf, base, s, d, send, recv):
        slot = base + lax.rem(z + (NZ - s if d == 0 else s), NZ)
        return remote(
            buf.at[slot],
            buf.at[slot],
            send.at[d, s],
            recv.at[d, s],
            z_up if d == 0 else z_dn,
            head,
        )

    def ring_in(buf, base, s, d, send, recv):
        slot = base + lax.rem(z + (NZ - s - 1 if d == 0 else s + 1), NZ)
        return remote(
            buf.at[slot],
            buf.at[slot],
            send.at[d, s],
            recv.at[d, s],
            z_up if d == 0 else z_dn,
            head,
        )

    land_ring = functools.partial(ring, land_all, y * NZ)
    land_in = functools.partial(ring_in, land_all, y * NZ)
    w_ring = [functools.partial(ring, b, 0) for b in lanes]
    w_in = [functools.partial(ring_in, b, 0) for b in lanes]
    def spread_land(zz):
        for dy in range(1, NY):
            ref = land_all.at[y * NZ + zz]
            to = lax.rem(y + dy, NY) * NZ + z
            remote(ref, ref, yl_s.at[dy], yl_r.at[dy], to, head).start()

    def lane_rows(lane):
        return pl.ds(0, LANE_ROWS[1]) if lane else pl.ds(LANE_ROWS[1], LANE_ROWS[0])

    def spread_weights(lane, zz):
        src = lanes[lane].at[zz]
        half_of = lax.div(zz, NZ // 2)
        dst = w_all.at[y, lax.rem(zz, NZ // 2), lane_rows(lane)]
        taker = 2 * x + half_of
        for dy in range(1, NY):
            to = lax.rem(y + dy, NY) * NZ + z
            remote(src, dst, yw_s.at[dy], yw_r.at[lane, dy], to, taker).start()

        @pl.when(half_of == lane)
        def _():
            pltpu.make_async_copy(src, dst, core_sem.at[2]).start()

        @pl.when(half_of != lane)
        def _():
            remote(src, dst, core_sem.at[0], core_sem.at[1], ctx, mate).start()

    for d in (0, 1):
        land_ring(0, d, land_s, land_r).start()
    @pl.when(off_diag)
    def _():
        on_lane(lambda lane: swap_main(lane).start())

    @pl.when(core == 0)
    def _():
        swap_lent.start()

    own_picks = pltpu.make_async_copy(pick_row, pick_all.at[ctx], pick_sem.at[1])
    own_picks.start()

    def tell(i, carry):
        remote(
            pick_row,
            pick_all.at[ctx],
            pick_sem.at[0],
            pick_sem.at[1],
            peer(NCTX - i),
            head,
        ).start()
        return carry

    lax.fori_loop(1, NCTX, tell, 0, unroll=True)

    spread_land(z)

    @pl.when(off_diag)
    def _():
        on_lane(lambda lane: swap_main(lane).wait_recv())

    @pl.when(core == 1)
    def _():
        swap_lent.wait_recv()

    @on_lane
    def _(lane):
        for d in (0, 1):
            w_ring[lane](0, d, wz_s, wz_r).start()
        spread_weights(lane, z)

    pltpu.make_async_copy(pick_all, pick_all, pick_sem.at[1]).wait()
    asked = pick_all[:, 0, :]
    lane = lax.broadcasted_iota(jnp.int32, asked.shape, 1)
    mine = jnp.logical_and(lane < GROUPS * HEADS * PICKS, (asked >> 4) == ctx)
    code = jnp.where(mine, (asked & 15) + ((lane >> 2) & 3) * BLOCKS, 0)
    code = jnp.max(code, axis=1, keepdims=True)
    code_v[...] = jnp.broadcast_to(code, code_v.shape)
    to_scalar = pltpu.make_async_copy(code_v, code_s, code_sem.at[0])
    to_scalar.start()
    to_scalar.wait()

    def block_for(cache, t):
        return cache[code_s[t, 0]]

    for c in loads[2:]:
        c.wait()
    recv_k[0] = block_for(pair_k, ctx)
    recv_v[0] = block_for(pair_v, ctx)

    def send_block(cache, out_buf, in_buf, which, j, carry):
        t, i = peer(j), slot_of(*offsets(j))
        out_buf[i] = block_for(cache, t)
        remote(
            out_buf.at[i], in_buf.at[i], kv_s.at[which], kv_r.at[which], t, head
        ).start()
        return carry

    send_key = functools.partial(send_block, pair_k, send_k, recv_k, 0)
    send_value = functools.partial(send_block, pair_v, send_v, recv_v, 1)

    def send_blocks(first, last):
        cut = NCTX - 1
        if first < cut:
            lax.fori_loop(first + 1, min(last, cut) + 1, send_key, 0)
        if last > cut:
            lax.fori_loop(max(first, cut) - cut + 1, last - cut + 1, send_value, 0)

    for s in range(STEPS):
        for d in (0, 1):
            if d == 0 or s < STEPS - 1:
                land_in(s, d, land_s, land_r).wait_recv()
                nxt = s + 1
                if nxt < STEPS - d:
                    land_ring(nxt, d, land_s, land_r).start()
                zz = lax.rem(z + (NZ - nxt if d == 0 else nxt), NZ)
                spread_land(zz)

                @on_lane
                def _(lane):
                    w_in[lane](s, d, wz_s, wz_r).wait_recv()
                    if nxt < STEPS - d:
                        w_ring[lane](nxt, d, wz_s, wz_r).start()
                    spread_weights(lane, zz)

        send_blocks(PER_STEP * s, PER_STEP * (s + 1))

    send_blocks(PER_STEP * STEPS, 2 * (NCTX - 1))

    def row_wait(buf, sem, row, n):
        ref = buf.at[pl.ds(row * n, n)]
        pltpu.make_async_copy(ref, ref, sem).wait()

    for dy in range(1, NY):
        row_wait(land_all, yl_r.at[dy], lax.rem(y + NY - dy, NY), NZ)

    def first_part(i, carry):
        g, h = lax.div(i, HEADS), lax.rem(i, HEADS)
        rows = pl.ds(pl.multiple_of(g * BLOCK, BLOCK), BLOCK)
        cols = pl.ds(pl.multiple_of(h * DH, DH), DH)
        qv = q[rows, cols]
        lk = land_all[:, 0:LAND, cols].reshape(NCTX * LAND, DH)
        lv = land_all[:, LAND : 2 * LAND, cols].reshape(NCTX * LAND, DH)
        s_l = lax.dot_general(qv, lk, NT, preferred_element_type=jnp.float32) * SCALE
        s_s = (
            lax.dot_general(
                qv, sk[rows, cols], NT, preferred_element_type=jnp.float32
            )
            * SCALE
        )
        causal = lax.broadcasted_iota(jnp.int32, s_s.shape, 0) >= lax.broadcasted_iota(
            jnp.int32, s_s.shape, 1
        )
        s_s = jnp.where(causal, s_s, -jnp.inf)
        m = jnp.maximum(
            jnp.max(s_l, axis=1, keepdims=True), jnp.max(s_s, axis=1, keepdims=True)
        )
        p_l, p_s = jnp.exp(s_l - m), jnp.exp(s_s - m)
        total = jnp.sum(p_l, axis=1, keepdims=True) + jnp.sum(
            p_s, axis=1, keepdims=True
        )
        acc[i] = jnp.dot(
            p_l.astype(jnp.bfloat16), lv, preferred_element_type=jnp.float32
        ) + jnp.dot(
            p_s.astype(jnp.bfloat16),
            sv[rows, cols],
            preferred_element_type=jnp.float32,
        )
        top[i] = jnp.broadcast_to(m, (BLOCK, DH))
        tot[i] = jnp.broadcast_to(total, (BLOCK, DH))
        return carry

    lax.fori_loop(0, GROUPS * HEADS, first_part, 0)


    def chosen(buf, i):
        blocks = []
        for p in range(PICKS):
            owner = picks[lax.div(i, HEADS), lax.rem(i, HEADS), p] >> 4
            slot = slot_of((y - (owner >> 4)) & 3, (z - (owner & 15)) & 15)
            blocks.append(buf[slot])
        return jnp.concatenate(blocks, axis=0)

    def kv_wait(buf, sem):
        ref = buf.at[pl.ds(1, NCTX - 1)]
        pltpu.make_async_copy(ref, ref, sem).wait()

    kv_wait(recv_k, kv_r.at[0])

    def second_part(i, carry):
        g, h = lax.div(i, HEADS), lax.rem(i, HEADS)
        rows = pl.ds(pl.multiple_of(g * BLOCK, BLOCK), BLOCK)
        cols = pl.ds(pl.multiple_of(h * DH, DH), DH)
        s = (
            lax.dot_general(
                q[rows, cols],
                chosen(recv_k, i),
                NT,
                preferred_element_type=jnp.float32,
            )
            * SCALE
        )
        m_old = top[i][:, :1]
        m = jnp.maximum(m_old, jnp.max(s, axis=1, keepdims=True))
        p = jnp.exp(s - m)
        shrink = jnp.exp(m_old - m)
        prob[i] = p.astype(jnp.bfloat16)
        acc[i] = acc[i] * shrink
        total = tot[i][:, :1] * shrink + jnp.sum(p, axis=1, keepdims=True)
        tot[i] = jnp.broadcast_to(total, (BLOCK, DH))
        return carry

    lax.fori_loop(0, GROUPS * HEADS, second_part, 0)
    def bytes_wait(ref, sem):
        pltpu.make_async_copy(ref, ref, sem).wait()

    for dy in range(1, NY):
        for lane in (0, 1):
            bytes_wait(
                w_all.at[lax.rem(y + NY - dy, NY), :, lane_rows(lane)],
                yw_r.at[lane, dy],
            )

    @on_lane
    def _(lane):
        bytes_wait(w_all.at[y, :, lane_rows(lane)], core_sem.at[2])
        bytes_wait(w_all.at[y, :, lane_rows(1 - lane)], core_sem.at[1])

    kv_wait(recv_v, kv_r.at[1])

    def att_copy(h, g, send, recv, to, half=None):
        rows = (
            pl.ds(g * BLOCK, BLOCK)
            if half is None
            else pl.ds(g * BLOCK + half * (BLOCK // 2), BLOCK // 2)
        )
        ref = att.at[h, rows]
        return remote(ref, ref, send, recv, ctx, to)

    started = []

    def go(c):
        c.start()
        started.append(c)

    up_lane, dn_lane, far_lane = 2 * x_up + core, 2 * x_dn + core, 2 * x_far + core
    up_mate, dn_mate = 2 * x_up + 1 - core, 2 * x_dn + 1 - core
    far_mate = 2 * x_far + 1 - core
    for g in range(GROUPS):
        for h in range(HEADS):
            i = g * HEADS + h
            total = acc[i] + jnp.dot(
                prob[i], chosen(recv_v, i), preferred_element_type=jnp.float32
            )
            att[head, g * BLOCK : (g + 1) * BLOCK, h * DH : (h + 1) * DH] = (
                total / tot[i]
            ).astype(jnp.bfloat16)
        go(att_copy(head, g, xs_s.at[0, g], xs_r.at[0, g], up_lane))
        go(att_copy(head, g, xs_s.at[1, g], xs_r.at[1, g], dn_lane))
        go(att_copy(head, g, mate_s.at[g], mate_r.at[g], mate))

    def add(h, first=False):
        prod = lax.dot_general(
            att[h],
            w_all[
                lax.div(h, 2),
                :,
                pl.ds(pl.multiple_of((1 - lax.rem(h, 2)) * BLOCK, BLOCK), BLOCK),
            ].reshape(WIDTH, WIDTH),
            NT,
            preferred_element_type=jnp.float32,
        )
        if first:
            sums[...] = prod
        else:
            sums[...] += prod

    def forward(g, d):
        lane_of = dn_lane if d == 0 else up_lane
        att_copy(lane_of, g, xs_s.at[d, g], xs_r.at[d, g], mate).wait_recv()
        to = up_lane if d == 0 else dn_lane
        go(att_copy(lane_of, g, far_s.at[d, g], far_r.at[d, g], to, half=d))
        go(att_copy(lane_of, g, fwd_s.at[d, g], fwd_r.at[d, g], mate))

    for g in range(GROUPS):
        for d in (0, 1):
            forward(g, d)
    add(head, first=True)
    for g in range(GROUPS):
        att_copy(mate, g, mate_s.at[g], mate_r.at[g], mate).wait_recv()
    for g in range(GROUPS):
        for d in (0, 1):
            att_copy(
                far_lane, g, far_s.at[d, g], far_r.at[d, g], mate, half=d
            ).wait_recv()
        go(att_copy(far_lane, g, ffw_s.at[g], ffw_r.at[g], mate))
    add(mate)
    add(dn_lane)
    add(up_lane)
    for d, h in ((0, dn_mate), (1, up_mate)):
        for g in range(GROUPS):
            att_copy(h, g, fwd_s.at[d, g], fwd_r.at[d, g], mate).wait_recv()
        add(h)
    add(far_lane)
    for g in range(GROUPS):
        att_copy(far_mate, g, ffw_s.at[g], ffw_r.at[g], mate).wait_recv()
    add(far_mate)
    out[...] = sums[...].astype(jnp.bfloat16)

    for c in started:
        c.wait_send()
    kv_wait(send_k, kv_s.at[0])
    kv_wait(send_v, kv_s.at[1])
    for dy in range(1, NY):
        row_wait(land_all, yl_s.at[dy], y, NZ)

    @on_lane
    def _(lane):
        for dy in range(1, NY):
            bytes_wait(lanes[lane], yw_s.at[dy])
        bytes_wait(lanes[lane].at[pl.ds(0, NZ // 2)], core_sem.at[0])

    for s in range(STEPS):
        for d in (0, 1):
            if s < STEPS - d:
                land_ring(s, d, land_s, land_r).wait_send()

    @on_lane
    def _(lane):
        for s in range(STEPS):
            for d in (0, 1):
                if s < STEPS - d:
                    w_ring[lane](s, d, wz_s, wz_r).wait_send()

    rest = pick_all.at[pl.ds(1, NCTX - 1)]
    pltpu.make_async_copy(rest, rest, pick_sem.at[0]).wait()

    @pl.when(off_diag)
    def _():
        on_lane(lambda lane: swap_main(lane).wait_send())

    @pl.when(core == 0)
    def _():
        swap_lent.wait_send()


def local(
    queries,
    span_keys,
    span_values,
    cache_keys,
    cache_values,
    land_keys,
    land_values,
    out_weight,
    selection,
):
    bf16, f32, i32 = jnp.bfloat16, jnp.float32, jnp.int32
    vmem = pl.BlockSpec(memory_space=pltpu.VMEM)
    dma = pltpu.SemaphoreType.DMA
    pairs = GROUPS * HEADS
    return pl.pallas_call(
        kernel,
        out_shape=jax.ShapeDtypeStruct((ROWS, WIDTH), bf16),
        in_specs=[pl.BlockSpec(memory_space=pltpu.SMEM)]
        + [pl.BlockSpec(memory_space=pl.ANY)] * 8,
        out_specs=vmem,
        scratch_shapes=[
            pltpu.VMEM((1, 128), i32),
            pltpu.VMEM((NCTX, 1, 128), i32),
            pltpu.VMEM((NCTX, 128), i32),
            pltpu.SMEM((NCTX, 128), i32),
            pltpu.VMEM((ROWS, WIDTH), bf16),
            pltpu.VMEM((ROWS, WIDTH), bf16),
            pltpu.VMEM((ROWS, WIDTH), bf16),
            pltpu.VMEM((NCTX, 2 * LAND, WIDTH), bf16),
            pltpu.VMEM((NZ, LANE_ROWS[0], WIDTH), bf16),
            pltpu.VMEM((NZ, LANE_ROWS[1], WIDTH), bf16),
            pltpu.VMEM((NY, NZ // 2, 2 * BLOCK, WIDTH), bf16),
            pltpu.VMEM((NCTX, BLOCK, DH), bf16),
            pltpu.VMEM((NCTX, BLOCK, DH), bf16),
            pltpu.VMEM((NCTX, BLOCK, DH), bf16),
            pltpu.VMEM((NCTX, BLOCK, DH), bf16),
            pltpu.VMEM((8, ROWS, WIDTH), bf16),
            pltpu.VMEM((pairs, BLOCK, PICKS * BLOCK), bf16),
            pltpu.VMEM((pairs, BLOCK, DH), f32),
            pltpu.VMEM((pairs, BLOCK, DH), f32),
            pltpu.VMEM((pairs, BLOCK, DH), f32),
            pltpu.VMEM((ROWS, WIDTH), f32),
            pltpu.VMEM((BLOCKS * HEADS, BLOCK, DH), bf16),
            pltpu.VMEM((BLOCKS * HEADS, BLOCK, DH), bf16),
            dma((2,)),
            dma((1,)),
            dma((13,)),
            dma((2, STEPS)),
            dma((2, STEPS)),
            dma((4,)),
            dma((2, STEPS)),
            dma((2, STEPS)),
            dma((3,)),
            dma((4,)),
            dma((4,)),
            dma((4,)),
            dma((2, 4)),
            dma((2,)),
            dma((2,)),
            dma((GROUPS,)),
            dma((GROUPS,)),
            dma((2, GROUPS)),
            dma((2, GROUPS)),
            dma((2, GROUPS)),
            dma((2, GROUPS)),
            dma((2, GROUPS)),
            dma((2, GROUPS)),
            dma((GROUPS,)),
            dma((GROUPS,)),
        ],
        compiler_params=pltpu.CompilerParams(
            collective_id=0, has_side_effects=True, vmem_limit_bytes=56 << 20
        ),
        name="landmark_attention",
    )(
        selection,
        queries,
        span_keys,
        span_values,
        cache_keys.reshape(BLOCKS, BLOCK, WIDTH),
        cache_values.reshape(BLOCKS, BLOCK, WIDTH),
        land_keys,
        land_values,
        out_weight.T,
    )


def solution(mesh):
    in_specs = (P("ctx", "head"),) * 7 + (P("head", "ctx"), P("ctx", "head", None))
    return jax.shard_map(
        local, mesh=mesh, in_specs=in_specs, out_specs=P("ctx", "head"), check_vma=False
    )
```
